512 devices in a mesh: hi: 16 (over z_lo, y), lo: 32 (over z_hi, x, core).
Axes of the slice: x: 4, y: 8, z: 8 (z_hi: 4, z_lo: 2; z = z_hi * 2 + z_lo), core: 2. Of those that a mesh axis runs over, the one named last changes fastest.
Arguments:
- state: float32 [16, 32, 262144], P('hi', 'lo'), may hold values from -6 to 6
- layer_angles: float32 [2, 2, 3, 6], replicated, may hold values from -3.140625 to 3.140625
- global_angles: float32 [2], replicated, may hold values from -3.140625 to 3.140625
Outputs:
- final_state: float32 [16, 32, 262144], P('hi', 'lo')
The draws below stay inside these ranges and needn't reach their ends.
All inputs are finite; a program needn't handle non-finite values.
Results may differ from the reference program's by a relative error of at most 0.00012.
Values sent between devices are 32-bit elements; how exact they have to be, the bound alone decides.
No kernel may reach another device: no remote copies, remote signals or barrier semaphores. Data moves between devices by JAX's collectives and lax.ppermute only.
A program may use at most 64 MiB of HBM per device.

```python
import jax
import jax.numpy as jnp
from jax import lax

QB = 6
DEPTH = 2
G = 64
LOCAL = 262144
N_HI = 16
N_LO = 32


def levels(key, extent, split, smallest, top_value):
    factor_of = 1.0
    for axis_at, shards_of in split:
        heights = jax.random.uniform(jax.random.fold_in(jax.random.fold_in(key, 6), axis_at), (shards_of,), jnp.float32, smallest / len(split), top_value / len(split))
        factor_of = factor_of * jnp.repeat(jnp.exp(heights), extent[axis_at] // shards_of).reshape((-1,) + (1,) * (len(extent) - 1 - axis_at))
    return factor_of


def centred(rng, dims, scale, bound, cuts=(), held_as=jnp.bfloat16):
    array = scale * jax.random.normal(rng, dims, jnp.float32)
    if cuts:
        array = array * levels(rng, dims, cuts, -0.22, 0.18)
    return jnp.clip(array, -bound, bound).astype(held_as)


def setup_inputs(seed: int = 0) -> dict:
    key_of = jax.random.split(jax.random.key(seed), 4)
    state = centred(key_of[0], (N_HI, N_LO, LOCAL), 1.0, 6.0, ((0, 16), (1, 32)), jnp.float32)
    layer_angles = jnp.clip(jax.random.uniform(key_of[1], (2, DEPTH, 3, QB), jnp.float32, -3.140625, 3.140625), -3.140625, 3.140625)
    global_angles = jnp.clip(jax.random.uniform(key_of[2], (2,), jnp.float32, -3.140625, 3.140625), -3.140625, 3.140625)
    return dict(state=state, layer_angles=layer_angles, global_angles=global_angles)


def merged_gates(angles):
    row_ids = jnp.arange(G, dtype=jnp.int32)
    cosines = jnp.cos(angles * 0.5)
    sines = jnp.sin(angles * 0.5)
    result = jnp.ones((3, G, G), dtype=angles.dtype)
    ladder = jnp.zeros((G,), dtype=jnp.int32)
    for qubit in range(QB):
        row_bit = (row_ids // (2 ** (QB - 1 - qubit))) % 2
        left_bit = row_bit[:, None]
        right_bit = row_bit[None, :]
        signed = jnp.where(left_bit == 1, 1.0, -1.0).astype(angles.dtype)
        entry = jnp.where((left_bit == right_bit)[None], cosines[:, qubit][:, None, None], signed[None] * sines[:, qubit][:, None, None])
        result = result * entry
        if qubit + 1 < QB:
            next_bit = (row_ids // (2 ** (QB - 2 - qubit))) % 2
            ladder = ladder + row_bit * next_bit
    parity = (1 - 2 * (ladder % 2)).astype(angles.dtype)
    return result * parity[None, :, None]


def cross_signs(dtype):
    row_ids = jnp.arange(G, dtype=jnp.int32)
    low_bit = row_ids % 2
    high_bit = row_ids // (G // 2)
    count = low_bit[:, None, None] * high_bit[None, :, None] + low_bit[None, :, None] * high_bit[None, None, :]
    return (1 - 2 * (count % 2)).astype(dtype)


def apply_section(amps, section_angles):
    ladder = cross_signs(amps.dtype)
    for layer in range(DEPTH):
        gates = merged_gates(section_angles[layer])
        amps = jnp.einsum('ad,ndbc->nabc', gates[0], amps, precision=lax.Precision.HIGHEST)
        amps = jnp.einsum('bd,nadc->nabc', gates[1], amps, precision=lax.Precision.HIGHEST)
        amps = jnp.einsum('cd,nabd->nabc', gates[2], amps, precision=lax.Precision.HIGHEST)
        amps = amps * ladder[None]
    return amps


def rotate_high(amps, angle, bit):
    blocks = 2 ** bit
    paired = amps.reshape(N_HI // (2 * blocks), 2, blocks, N_LO, LOCAL)
    cosine = jnp.cos(angle * 0.5)
    sine = jnp.sin(angle * 0.5)
    lower = paired[:, 0]
    upper = paired[:, 1]
    joined = jnp.stack([cosine * lower - sine * upper, sine * lower + cosine * upper], axis=1)
    return joined.reshape(N_HI, N_LO, LOCAL)


def reference(state, layer_angles, global_angles):
    amps = apply_section(state.reshape(N_HI * N_LO, G, G, G), layer_angles[0]).reshape(N_HI, N_LO, LOCAL)
    amps = rotate_high(amps, global_angles[0], 0)
    amps = amps.reshape(N_HI, N_LO, N_LO, LOCAL // N_LO).transpose(0, 2, 1, 3).reshape(N_HI, N_LO, LOCAL)
    amps = apply_section(amps.reshape(N_HI * N_LO, G, G, G), layer_angles[1]).reshape(N_HI, N_LO, LOCAL)
    return rotate_high(amps, global_angles[1], N_HI.bit_length() - 2)
```

```python
import functools

import jax
import jax.numpy as jnp
from jax import lax
from jax.experimental import pallas as pl
from jax.experimental.pallas import tpu as pltpu
from jax.sharding import Mesh
from jax.sharding import PartitionSpec as P

ROW_BITS = (1, 2, 3, 4, 7, 8, 9, 10)
COL_BITS = (0, 11, 12, 13, 14, 15, 16, 17)
SIDE = 256
CHUNKS = 4
BLOCKS = 32
ROWS = 16
LANES = 128


def trig(angles_ref, section, layer):
    half = angles_ref[section, layer] * 0.5
    cosines, sines = jnp.cos(half), jnp.sin(half)

    def of(bit):
        group, qubit = bit // 6, bit % 6
        return (
            cosines[group : group + 1, qubit : qubit + 1],
            sines[group : group + 1, qubit : qubit + 1],
        )

    return of


def bit_of(index, place):
    return (index >> place) & 1


def gate_tiles(bits, of, transposed, skip=()):
    row = lax.broadcasted_iota(jnp.int32, (8, LANES), 0)
    lane = lax.broadcasted_iota(jnp.int32, (8, LANES), 1)
    pairs = [
        (i, i + 1)
        for i in range(7)
        if bits[i] + 1 == bits[i + 1] and not {bits[i], bits[i + 1]} & set(skip)
    ]

    def entry(bit, r, c):
        if bit in skip:
            if isinstance(r, int) and isinstance(c, int):
                return 1.0 if r == c else 0.0
            return jnp.where(r == c, 1.0, 0.0)
        cosine, sine = of(bit)
        out, inner = (c, r) if transposed else (r, c)
        if isinstance(r, int) and isinstance(c, int):
            return cosine if out == inner else sine if out == 1 else -sine
        return jnp.where(r == c, cosine, jnp.where(out == 1, sine, -sine))

    base = jnp.ones((8, LANES), jnp.float32)
    for i in (5, 6, 7):
        base = base * entry(bits[i], bit_of(row, 7 - i), bit_of(lane, 7 - i))
    out_bit = {i: bit_of(lane if transposed else row, 7 - i) for i in (range(1, 8) if transposed else range(5, 8))}
    parity = jnp.zeros((8, LANES), jnp.int32)
    for i, j in pairs:
        if i in out_bit and j in out_bit:
            parity = parity + out_bit[i] * out_bit[j]
    base = base * (1 - 2 * (parity & 1)).astype(jnp.float32)
    tiles = {(): base}
    for i in (4, 3, 2, 1):
        grown = {}
        for r in (0, 1):
            factor = entry(bits[i], r, bit_of(lane, 7 - i))
            if not transposed and r == 1 and (i, i + 1) in pairs and i + 1 in out_bit:
                factor = factor * (1 - 2 * out_bit[i + 1]).astype(jnp.float32)
            for key, tile in tiles.items():
                grown[(r, *key)] = tile * factor
        tiles = grown
    halves = []
    for c in (0, 1):
        column = {}
        for r in (0, 1):
            factor = entry(bits[0], r, c)
            if transposed and c == 1 and (0, 1) in pairs:
                factor = factor * (1 - 2 * out_bit[1]).astype(jnp.float32)
            for key, tile in tiles.items():
                column[(r, *key)] = tile * factor
        if not transposed:
            for key in column:
                flips = sum(key[i] * key[j] for i, j in pairs if i < 5 and j < 5)
                if flips % 2:
                    column[key] = -column[key]
        halves.append(jnp.concatenate([column[key] for key in sorted(column)], axis=0))
    return jnp.concatenate(halves, axis=1)


def split(value):
    high = value.astype(jnp.bfloat16)
    low = (value - high.astype(jnp.float32)).astype(jnp.bfloat16)
    return high, low


def dot3(left, right):
    mul = functools.partial(jnp.dot, preferred_element_type=jnp.float32)
    return mul(left[0], right[0]) + mul(left[0], right[1]) + mul(left[1], right[0])


def chunk_gates(angles_ref, section):
    first, later = trig(angles_ref, section, 0), trig(angles_ref, section, 1)
    return (
        split(gate_tiles(ROW_BITS, first, False)),
        split(gate_tiles(COL_BITS, first, True)),
        split(gate_tiles(ROW_BITS, later, False, skip=(4, 7))),
        split(gate_tiles(COL_BITS, later, True)),
    )


def cross_sign():
    row = lax.broadcasted_iota(jnp.int32, (SIDE, SIDE), 0)
    column = lax.broadcasted_iota(jnp.int32, (SIDE, SIDE), 1)
    parity = bit_of(row, 7) * bit_of(column, 7) + bit_of(row, 0) * bit_of(column, 6)
    return (1 - 2 * (parity & 1)).astype(jnp.float32)


def chunk_layers(chunk, gates, sign):
    left0, right0, left1, right1 = gates
    chunk = dot3(split(chunk), right0)
    chunk = dot3(left0, split(chunk)) * sign
    chunk = dot3(split(chunk), right1)
    return dot3(left1, split(chunk)) * sign


def finish_section(angles_ref, section, load, store):
    first, later = trig(angles_ref, section, 0), trig(angles_ref, section, 1)
    wide = lambda pair: tuple(jnp.broadcast_to(v, (8, LANES)) for v in pair)
    first = {bit: wide(first(bit)) for bit in (5, 6)}
    later = {bit: wide(later(bit)) for bit in (4, 5, 6, 7)}
    row = lax.broadcasted_iota(jnp.int32, (8, LANES), 0)
    flip8 = (1 - 2 * bit_of(row, 2)).astype(jnp.float32)

    def rotate(tiles, signs, place, pair):
        cosine, sine = pair
        for key in list(tiles):
            if key[place]:
                continue
            other = (*key[:place], 1, *key[place + 1 :])
            x, y = tiles[key], tiles[other]
            if signs[key] == signs[other]:
                tiles[key], tiles[other] = cosine * x - sine * y, sine * x + cosine * y
            else:
                tiles[key], tiles[other] = cosine * x + sine * y, sine * x - cosine * y
            signs[other] = signs[key]

    def group(base, b3):
        keys = [(b4, b5, b6, b7) for b4 in (0, 1) for b5 in (0, 1) for b6 in (0, 1) for b7 in (0, 1)]
        tiles = {key: load(key[1] * 2 + key[2], base + key[0], key[3]) for key in keys}
        signs = dict.fromkeys(keys, 1)
        rotate(tiles, signs, 1, first[5])
        rotate(tiles, signs, 2, first[6])
        for key in keys:
            b4, b5, b6, b7 = key
            signs[key] *= (-1) ** (b4 * b5 + b5 * b6 + b6 * b7)
        for place, bit in enumerate((4, 5, 6, 7)):
            rotate(tiles, signs, place, later[bit])
        for key in keys:
            b4, b5, b6, b7 = key
            sign = signs[key] * (-1) ** (b3 * b4 + b4 * b5 + b5 * b6 + b6 * b7)
            value = tiles[key]
            if b7:
                value = value * (flip8 if sign == 1 else -flip8)
            elif sign == -1:
                value = -value
            store(b5 * 2 + b6, base + b4, b7, value)

    @pl.loop(0, 8)
    def _(step):
        group(step * 4, 0)
        group(step * 4 + 2, 1)


def half_rows(b7):
    return pl.ds(b7 * 8, 8)


def first_kernel(angles_ref, state_ref, out_ref):
    gates = chunk_gates(angles_ref, 0)
    sign = cross_sign()
    for c in range(CHUNKS):
        chunk = jnp.concatenate(
            [state_ref[half * 16 : half * 16 + 16, c].reshape(SIDE, LANES) for half in (0, 1)], axis=1
        )
        chunk = chunk_layers(chunk, gates, sign)
        for half in (0, 1):
            out_ref[c, half * 16 : half * 16 + 16] = chunk[:, half * LANES : (half + 1) * LANES].reshape(16, ROWS, LANES)

    def load(c, block, b7):
        return out_ref[c, block, half_rows(b7)]

    def store(c, block, b7, value):
        out_ref[c, block, half_rows(b7)] = value

    finish_section(angles_ref, 0, load, store)


def middle_kernel(angles_ref, global_ref, in_ref, out_ref):
    gates = chunk_gates(angles_ref, 1)
    sign = cross_sign()
    half = global_ref[...] * 0.5
    cosines, sines = jnp.cos(half), jnp.sin(half)
    low, high = ((cosines[:, i : i + 1], sines[:, i : i + 1]) for i in (0, 1))

    def entry(pair, out, inner):
        return pair[0] if out == inner else pair[1] if out == 1 else -pair[1]

    for c in range(CHUNKS):
        halves = []
        for side in (0, 1):
            total = None
            for source in range(CHUNKS):
                factor = entry(high, c >> 1, source >> 1) * entry(low, c & 1, source & 1)
                term = factor * in_ref[source, side * 16 : side * 16 + 16].reshape(SIDE, LANES)
                total = term if total is None else total + term
            halves.append(total)
        chunk = chunk_layers(jnp.concatenate(halves, axis=1), gates, sign)
        for side in (0, 1):
            out_ref[c, side * 16 : side * 16 + 16] = chunk[:, side * LANES : (side + 1) * LANES].reshape(16, ROWS, LANES)


def last_kernel(angles_ref, in_ref, out_ref):
    def load(c, block, b7):
        return in_ref[c, block, half_rows(b7)]

    def store(c, block, b7, value):
        out_ref[block, c, half_rows(b7)] = value

    finish_section(angles_ref, 1, load, store)


VMEM = pl.BlockSpec(memory_space=pltpu.VMEM)


def call(kernel, shape, *args):
    return pl.pallas_call(
        kernel,
        out_shape=jax.ShapeDtypeStruct(shape, jnp.float32),
        in_specs=[VMEM] * len(args),
        out_specs=VMEM,
        compiler_params=pltpu.CompilerParams(vmem_limit_bytes=32 * 2**20),
    )(*args)


def on_device(state, layer_angles, global_angles):
    by_chunk = (CHUNKS, BLOCKS, ROWS, LANES)
    amps = call(first_kernel, by_chunk, layer_angles, state.reshape(BLOCKS, CHUNKS, ROWS, LANES))
    amps = lax.all_to_all(
        amps.reshape(CHUNKS * BLOCKS, ROWS, LANES), ("h3", "h0", "lo"), split_axis=0, concat_axis=0, tiled=True
    )
    amps = call(middle_kernel, by_chunk, layer_angles, global_angles.reshape(1, 2), amps.reshape(by_chunk))
    amps = lax.all_to_all(
        amps.reshape(CHUNKS, BLOCKS * ROWS, LANES), ("h3", "h0"), split_axis=0, concat_axis=0, tiled=True
    )
    amps = call(last_kernel, (BLOCKS, CHUNKS, ROWS, LANES), layer_angles, amps.reshape(by_chunk))
    return amps.reshape(state.shape)


def solution(mesh):
    high, low = mesh.shape["hi"], mesh.shape["lo"]
    finer = Mesh(mesh.devices.reshape(2, high // 4, 2, low), ("h3", "hm", "h0", "lo"))
    spec = P(("h3", "hm", "h0"), "lo", None)
    return jax.shard_map(on_device, mesh=finer, in_specs=(spec, P(), P()), out_specs=spec, check_vma=False)
```

```python
import functools

import jax
import jax.numpy as jnp
from jax import lax
from jax.experimental import pallas as pl
from jax.experimental.pallas import tpu as pltpu
from jax.sharding import Mesh
from jax.sharding import PartitionSpec as P

ROW_BITS = (1, 2, 3, 4, 7, 8, 9, 10)
COL_BITS = (0, 11, 12, 13, 14, 15, 16, 17)
SIDE = 256
CHUNKS = 4
BLOCKS = 32
ROWS = 16
LANES = 128
TILE = (8, LANES)
MIB = 2**20
PARTS = 4


def trig(angles_ref, section, layer):
    half = angles_ref[section, :, layer] * 0.5
    cosines, sines = jnp.cos(half), jnp.sin(half)

    def of(bit):
        group, qubit = bit // 6, bit % 6
        return (
            cosines[group : group + 1, qubit : qubit + 1],
            sines[group : group + 1, qubit : qubit + 1],
        )

    return of


def bit_of(index, place):
    return (index >> place) & 1


def signs_of(parity):
    return (1 - 2 * (parity & 1)).astype(jnp.float32)


def ry(pair, out, inner):
    cosine, sine = pair
    if isinstance(out, int):
        return cosine if out == inner else sine if out == 1 else -sine
    return jnp.where(out == inner, cosine, jnp.where(out == 1, sine, -sine))


def gate(bits, of, transposed):
    row = lax.broadcasted_iota(jnp.int32, TILE, 0)
    lane = lax.broadcasted_iota(jnp.int32, TILE, 1)
    pairs = [(i, i + 1) for i in range(7) if bits[i] + 1 == bits[i + 1]]

    def entry(i, r, c):
        cosine, sine = of(bits[i])
        out, inner = (c, r) if transposed else (r, c)
        if isinstance(c, int):
            return ry((cosine, sine), out, inner)
        return jnp.where(r == c, cosine, jnp.where(out == 1, sine, -sine))

    if transposed:
        out_bit = {i: bit_of(lane, 7 - i) for i in range(1, 8)}
    else:
        out_bit = {i: bit_of(row, 7 - i) for i in range(5, 8)}
    base = jnp.ones(TILE, jnp.float32)
    for i in (5, 6, 7):
        base = base * entry(i, bit_of(row, 7 - i), bit_of(lane, 7 - i))
    parity = jnp.zeros(TILE, jnp.int32)
    for i, j in pairs:
        if i in out_bit and j in out_bit:
            parity = parity + out_bit[i] * out_bit[j]
    tiles = {(): base * signs_of(parity)}
    for i in (4, 3, 2, 1):
        grown = {}
        for r in (0, 1):
            factor = entry(i, r, bit_of(lane, 7 - i))
            if not transposed and r == 1 and (i, i + 1) in pairs and i + 1 in out_bit:
                factor = factor * signs_of(out_bit[i + 1])
            for key, tile in tiles.items():
                grown[(r, *key)] = tile * factor
        tiles = grown
    halves = []
    for c in (0, 1):
        column = {}
        for r in (0, 1):
            factor = entry(0, r, c)
            if transposed and c == 1 and (0, 1) in pairs:
                factor = factor * signs_of(out_bit[1])
            for key, tile in tiles.items():
                column[(r, *key)] = tile * factor
        if not transposed:
            for key in column:
                if sum(key[i] * key[j] for i, j in pairs if j < 5) % 2:
                    column[key] = -column[key]
        halves.append(jnp.concatenate([column[key] for key in sorted(column)], axis=0))
    return jnp.concatenate(halves, axis=1)


def split(value):
    high = value.astype(jnp.bfloat16)
    low = (value - high.astype(jnp.float32)).astype(jnp.bfloat16)
    return high, low


def dot3(left, right):
    mul = functools.partial(jnp.dot, preferred_element_type=jnp.float32)
    return mul(left[0], right[0]) + mul(left[0], right[1]) + mul(left[1], right[0])


def section_gates(angles_ref, section):
    gates = []
    for layer in (0, 1):
        of = trig(angles_ref, section, layer)
        gates.append(split(gate(COL_BITS, of, True)))
        gates.append(split(gate(ROW_BITS, of, False)))
    return gates


def edge_tile():
    row = lax.broadcasted_iota(jnp.int32, TILE, 0)
    lane = lax.broadcasted_iota(jnp.int32, TILE, 1)
    return signs_of(bit_of(row, 0) * bit_of(lane, 6))


def chunk_sign(tile_of):
    tiles = {(b4, b7): tile_of(b4, b7) for b4 in (0, 1) for b7 in (0, 1)}
    columns = []
    for b0 in (0, 1):
        column = []
        for upper in range(16):
            for b7 in (0, 1):
                tile = tiles[upper & 1, b7]
                column.append(-tile if b0 and upper >= 8 else tile)
        columns.append(jnp.concatenate(column, axis=0))
    return jnp.concatenate(columns, axis=1)


def chunk_layers(chunks, gates, signs0, sign1):
    right0, left0, right1, left1 = gates
    chunks = [dot3(split(chunk), right0) for chunk in chunks]
    chunks = [dot3(left0, split(chunk)) * sign for chunk, sign in zip(chunks, signs0, strict=True)]
    chunks = [dot3(split(chunk), right1) for chunk in chunks]
    return [dot3(left1, split(chunk)) * sign1 for chunk in chunks]


def weighted(factors, values):
    total = None
    for factor, value in zip(factors, values, strict=True):
        term = factor * value
        total = term if total is None else total + term
    return total


def to_chunk(pieces):
    return jnp.concatenate([piece.reshape(SIDE, LANES) for piece in pieces], axis=1)


def of_chunk(chunk, half):
    return chunk[:, half * LANES : (half + 1) * LANES].reshape(16, ROWS, LANES)


def halves(half):
    return slice(half * 16, half * 16 + 16)


def outer_parity(b4, b5, b6, b7):
    return (b4 * b5 + b5 * b6 + b6 * b7) % 2


def first_kernel(angles_ref, state_ref, out_ref, angles, held, mixed, done):
    copies = [pltpu.make_async_copy(angles_ref, angles, done.at[PARTS])]
    for part in range(PARTS):
        span = pl.ds(part * BLOCKS // PARTS, BLOCKS // PARTS)
        copies.append(pltpu.make_async_copy(state_ref.at[span], held.at[span], done.at[part]))
    for copy in copies:
        copy.start()
    copies[0].wait()
    first, later, next_section = trig(angles, 0, 0), trig(angles, 0, 1), trig(angles, 1, 0)
    gates = section_gates(angles, 0)
    edge = edge_tile()
    sign1 = chunk_sign(lambda b4, b7: edge)
    for copy in copies[1:]:
        copy.wait()
    chunks, signs0 = [], []
    for c in range(CHUNKS):
        factors = [
            jnp.broadcast_to(ry(first(5), c >> 1, k >> 1) * ry(first(6), c & 1, k & 1), TILE) for k in range(CHUNKS)
        ]
        factors = [jnp.concatenate([f, f], axis=0)[None] for f in factors]
        chunks.append(to_chunk([weighted(factors, [held[halves(b0), k] for k in range(CHUNKS)]) for b0 in (0, 1)]))
        signs0.append(chunk_sign(lambda b4, b7: -edge if outer_parity(b4, c >> 1, c & 1, b7) else edge))
    chunks = chunk_layers(chunks, gates, signs0, sign1)
    for c, chunk in enumerate(chunks):
        for b0 in (0, 1):
            mixed[c, halves(b0)] = of_chunk(chunk, b0)
    later5, later6, next5, next6 = later(5), later(6), next_section(5), next_section(6)
    before = [[ry(later5, k >> 1, i >> 1) * ry(later6, k & 1, i & 1) for i in range(CHUNKS)] for k in range(CHUNKS)]
    after = [[ry(next5, o >> 1, k >> 1) * ry(next6, o & 1, k & 1) for k in range(CHUNKS)] for o in range(CHUNKS)]
    factors = {}
    for b4 in (0, 1):
        for b7 in (0, 1):
            for o in range(CHUNKS):
                for i in range(CHUNKS):
                    total = None
                    for k in range(CHUNKS):
                        term = after[o][k] * before[k][i]
                        if outer_parity(b4, k >> 1, k & 1, b7):
                            term = -term
                        total = term if total is None else total + term
                    factors[b4, b7, o, i] = jnp.broadcast_to(total, TILE)
    copies = []
    for part in range(PARTS):
        start = part * BLOCKS // PARTS
        for b4 in (0, 1):
            for b7 in (0, 1):
                rows = slice(b7 * 8, b7 * 8 + 8)
                for block in range(start + b4, start + BLOCKS // PARTS, 2):
                    tiles = [mixed[i, block, rows] for i in range(CHUNKS)]
                    for o in range(CHUNKS):
                        mixed[o, block, rows] = weighted([factors[b4, b7, o, i] for i in range(CHUNKS)], tiles)
        span = pl.ds(start, BLOCKS // PARTS)
        copies.append(pltpu.make_async_copy(mixed.at[:, span], out_ref.at[:, span], done.at[part]))
        copies[-1].start()
    for copy in copies:
        copy.wait()


def prepare_kernel(angles_ref, global_ref, gates_ref, spin_ref, sign_ref, last_ref):
    for at, (high, low) in enumerate(section_gates(angles_ref, 1)):
        gates_ref[at, 0] = high
        gates_ref[at, 1] = low
    place5, place6 = lax.axis_index("h3"), lax.axis_index("h0")
    half = global_ref[...] * 0.5
    cosines, sines = jnp.cos(half), jnp.sin(half)
    low, high = ((cosines[:, i : i + 1], sines[:, i : i + 1]) for i in (0, 1))
    later = trig(angles_ref, 1, 1)
    for o in range(CHUNKS):
        for k in range(CHUNKS):
            spin_ref[o, k] = jnp.broadcast_to(ry(high, o >> 1, k >> 1) * ry(low, o & 1, k & 1), TILE)
            last_ref[o, k] = jnp.broadcast_to(ry(later(5), o >> 1, k >> 1) * ry(later(6), o & 1, k & 1), TILE)
    edge = edge_tile()
    sign5, sign6 = signs_of(place5), signs_of(place6)
    both = signs_of(place5 * place6)
    for b4 in (0, 1):
        for b7 in (0, 1):
            factor = both
            if b4:
                factor = factor * sign5
            if b7:
                factor = factor * sign6
            sign_ref[b4, b7] = edge * factor


def middle_kernel(gates_ref, spin_ref, sign_ref, in_ref, out_ref):
    gates = [(gates_ref[at, 0], gates_ref[at, 1]) for at in range(4)]
    chunks = []
    for c in range(CHUNKS):
        factors = [jnp.concatenate([spin_ref[c, k]] * 2, axis=0)[None] for k in range(CHUNKS)]
        chunks.append(to_chunk([weighted(factors, [in_ref[k, halves(b0)] for k in range(CHUNKS)]) for b0 in (0, 1)]))
    edge = edge_tile()
    sign0 = chunk_sign(lambda b4, b7: sign_ref[b4, b7])
    chunks = chunk_layers(chunks, gates, [sign0] * CHUNKS, chunk_sign(lambda b4, b7: edge))
    for c, chunk in enumerate(chunks):
        for b0 in (0, 1):
            out_ref[c, halves(b0)] = of_chunk(chunk, b0)


def last_kernel(last_ref, in_ref, out_ref, held, done):
    factors = [[last_ref[o, k] for k in range(CHUNKS)] for o in range(CHUNKS)]
    size = BLOCKS // PARTS
    copies = []
    for part in range(PARTS):
        for block in range(part * size, part * size + size):
            for b7 in (0, 1):
                rows = slice(b7 * 8, b7 * 8 + 8)
                tiles = [in_ref[k, block, rows] for k in range(CHUNKS)]
                for o in range(CHUNKS):
                    value = weighted(factors[o], tiles)
                    held[block, o, rows] = -value if outer_parity(block & 1, o >> 1, o & 1, b7) else value
        span = pl.ds(part * size, size)
        copies.append(pltpu.make_async_copy(held.at[span], out_ref.at[span], done.at[part]))
        copies[-1].start()
    for copy in copies:
        copy.wait()


VMEM = pl.BlockSpec(memory_space=pltpu.VMEM)
HBM = pl.BlockSpec(memory_space=pltpu.HBM)
BY_CHUNK = (CHUNKS, BLOCKS, ROWS, LANES)
NATURAL = (BLOCKS, CHUNKS, ROWS, LANES)
CHUNK = (BLOCKS, ROWS, LANES)


def f32(*shape):
    return jax.ShapeDtypeStruct(shape, jnp.float32)


def call(kernel, out_shape, *args, specs=None, out_specs=VMEM, scratch=(), flops=0, limit=16):
    return pl.pallas_call(
        kernel,
        out_shape=out_shape,
        in_specs=specs or [VMEM] * len(args),
        out_specs=out_specs,
        scratch_shapes=scratch,
        cost_estimate=pl.CostEstimate(flops=flops, bytes_accessed=2 * MIB, transcendentals=0),
        compiler_params=pltpu.CompilerParams(vmem_limit_bytes=limit * MIB),
    )(*args)


def first_call(angles, state):
    return call(
        first_kernel, f32(*BY_CHUNK), angles, state, specs=[HBM, HBM], out_specs=HBM,
        scratch=[
            pltpu.VMEM(angles.shape, jnp.float32),
            pltpu.VMEM(NATURAL, jnp.float32),
            pltpu.VMEM(BY_CHUNK, jnp.float32),
            pltpu.SemaphoreType.DMA((PARTS + 1,)),
        ],
        flops=1600 * MIB, limit=62,
    )


def prepare_call(angles, global_angles):
    shapes = (
        jax.ShapeDtypeStruct((4, 2, SIDE, SIDE), jnp.bfloat16),
        f32(CHUNKS, CHUNKS, *TILE),
        f32(2, 2, *TILE),
        f32(CHUNKS, CHUNKS, *TILE),
    )
    return call(prepare_kernel, shapes, angles, global_angles, out_specs=(VMEM,) * 4, flops=400 * MIB)


def middle_call(gates, spin, sign, amps):
    return call(middle_kernel, f32(*BY_CHUNK), gates, spin, sign, amps, flops=1600 * MIB)


def last_call(last, amps):
    return call(
        last_kernel, f32(*NATURAL), last, amps, out_specs=HBM,
        scratch=[pltpu.VMEM(NATURAL, jnp.float32), pltpu.SemaphoreType.DMA((PARTS,))],
    )


def second_half(angles, global_angles, amps):
    gates, spin, sign, last = prepare_call(angles, global_angles.reshape(1, 2))
    amps = middle_call(gates, spin, sign, amps)
    amps = lax.all_to_all(
        amps.reshape(CHUNKS, BLOCKS * ROWS, LANES), ("h3", "h0"), split_axis=0, concat_axis=0, tiled=True
    )
    return last_call(last, amps.reshape(BY_CHUNK))


def on_device(state, layer_angles, global_angles):
    angles = layer_angles.transpose(0, 2, 1, 3)
    amps = first_call(angles, state.reshape(NATURAL))
    amps = lax.all_to_all(
        amps.reshape(CHUNKS * BLOCKS, ROWS, LANES), ("h3", "h0", "lo"), split_axis=0, concat_axis=0, tiled=True
    ).reshape(BY_CHUNK)
    return second_half(angles, global_angles, amps).reshape(state.shape)


def solution(mesh):
    high, low = mesh.shape["hi"], mesh.shape["lo"]
    finer = Mesh(mesh.devices.reshape(2, high // 4, 2, low), ("h3", "hm", "h0", "lo"))
    spec = P(("h3", "hm", "h0"), "lo", None)
    return jax.shard_map(on_device, mesh=finer, in_specs=(spec, P(), P()), out_specs=spec, check_vma=False)
```

```python
import functools

import jax
import jax.numpy as jnp
from jax import lax
from jax.experimental import pallas as pl
from jax.experimental.pallas import tpu as pltpu
from jax.sharding import Mesh
from jax.sharding import PartitionSpec as P

ROW_BITS = (1, 2, 3, 4, 7, 8, 9, 10)
COL_BITS = (0, 11, 12, 13, 14, 15, 16, 17)
SIDE = 256
CHUNKS = 4
BLOCKS = 32
ROWS = 16
LANES = 128
TILE = (8, LANES)
EVERY = [(o, i) for o in range(CHUNKS) for i in range(CHUNKS)]
MIB = 2**20
PARTS = 4


def trig(angles_ref, section, layer):
    half = angles_ref[section, :, layer] * 0.5
    cosines, sines = jnp.cos(half), jnp.sin(half)

    def of(bit):
        group, qubit = bit // 6, bit % 6
        return (
            cosines[group : group + 1, qubit : qubit + 1],
            sines[group : group + 1, qubit : qubit + 1],
        )

    return of


def bit_of(index, place):
    return (index >> place) & 1


def signs_of(parity):
    return (1 - 2 * (parity & 1)).astype(jnp.float32)


def ry(pair, out, inner):
    cosine, sine = pair
    if isinstance(out, int):
        return cosine if out == inner else sine if out == 1 else -sine
    return jnp.where(out == inner, cosine, jnp.where(out == 1, sine, -sine))


def gate(bits, of, transposed):
    row = lax.broadcasted_iota(jnp.int32, TILE, 0)
    lane = lax.broadcasted_iota(jnp.int32, TILE, 1)
    pairs = [(i, i + 1) for i in range(7) if bits[i] + 1 == bits[i + 1]]

    def entry(i, r, c):
        cosine, sine = of(bits[i])
        out, inner = (c, r) if transposed else (r, c)
        if isinstance(c, int):
            return ry((cosine, sine), out, inner)
        return jnp.where(r == c, cosine, jnp.where(out == 1, sine, -sine))

    if transposed:
        out_bit = {i: bit_of(lane, 7 - i) for i in range(1, 8)}
    else:
        out_bit = {i: bit_of(row, 7 - i) for i in range(5, 8)}
    base = jnp.ones(TILE, jnp.float32)
    for i in (5, 6, 7):
        base = base * entry(i, bit_of(row, 7 - i), bit_of(lane, 7 - i))
    parity = jnp.zeros(TILE, jnp.int32)
    for i, j in pairs:
        if i in out_bit and j in out_bit:
            parity = parity + out_bit[i] * out_bit[j]
    tiles = {(): base * signs_of(parity)}
    for i in (4, 3, 2, 1):
        grown = {}
        for r in (0, 1):
            factor = entry(i, r, bit_of(lane, 7 - i))
            if not transposed and r == 1 and (i, i + 1) in pairs and i + 1 in out_bit:
                factor = factor * signs_of(out_bit[i + 1])
            for key, tile in tiles.items():
                grown[(r, *key)] = tile * factor
        tiles = grown
    halves = []
    for c in (0, 1):
        column = {}
        for r in (0, 1):
            factor = entry(0, r, c)
            if transposed and c == 1 and (0, 1) in pairs:
                factor = factor * signs_of(out_bit[1])
            for key, tile in tiles.items():
                column[(r, *key)] = tile * factor
        if not transposed:
            for key in column:
                if sum(key[i] * key[j] for i, j in pairs if j < 5) % 2:
                    column[key] = -column[key]
        halves.append(jnp.concatenate([column[key] for key in sorted(column)], axis=0))
    return jnp.concatenate(halves, axis=1)


def split(value):
    high = value.astype(jnp.bfloat16)
    low = (value - high.astype(jnp.float32)).astype(jnp.bfloat16)
    return high, low


def dot3(left, right):
    mul = functools.partial(jnp.dot, preferred_element_type=jnp.float32)
    return mul(left[0], right[0]) + mul(left[0], right[1]) + mul(left[1], right[0])


def section_gates(angles_ref, section):
    gates = []
    for layer in (0, 1):
        of = trig(angles_ref, section, layer)
        gates.append(split(gate(COL_BITS, of, True)))
        gates.append(split(gate(ROW_BITS, of, False)))
    return gates


def edge_tile():
    row = lax.broadcasted_iota(jnp.int32, TILE, 0)
    lane = lax.broadcasted_iota(jnp.int32, TILE, 1)
    return signs_of(bit_of(row, 0) * bit_of(lane, 6))


def chunk_sign(tile_of):
    tiles = {(b4, b7): tile_of(b4, b7) for b4 in (0, 1) for b7 in (0, 1)}
    columns = []
    for b0 in (0, 1):
        column = []
        for upper in range(16):
            for b7 in (0, 1):
                tile = tiles[upper & 1, b7]
                column.append(-tile if b0 and upper >= 8 else tile)
        columns.append(jnp.concatenate(column, axis=0))
    return jnp.concatenate(columns, axis=1)


def chunk_layers(chunks, gates, signs0, sign1):
    right0, left0, right1, left1 = gates
    chunks = [dot3(split(chunk), right0) for chunk in chunks]
    chunks = [dot3(left0, split(chunk)) * sign for chunk, sign in zip(chunks, signs0, strict=True)]
    chunks = [dot3(split(chunk), right1) for chunk in chunks]
    return [dot3(left1, split(chunk)) * sign1 for chunk in chunks]


def weighted(factors, values):
    total = None
    for factor, value in zip(factors, values, strict=True):
        term = factor * value
        total = term if total is None else total + term
    return total


def to_chunk(pieces):
    return jnp.concatenate([piece.reshape(SIDE, LANES) for piece in pieces], axis=1)


def of_chunk(chunk, half):
    return chunk[:, half * LANES : (half + 1) * LANES].reshape(16, ROWS, LANES)


def halves(half):
    return slice(half * 16, half * 16 + 16)


def outer_parity(b4, b5, b6, b7):
    return (b4 * b5 + b5 * b6 + b6 * b7) % 2


def pair_of(first, second, out, inner):
    return ry(first, out >> 1, inner >> 1) * ry(second, out & 1, inner & 1)


def prepare_first(angles_ref):
    gates = section_gates(angles_ref, 0)
    angles = [trig(angles_ref, *at) for at in ((0, 0), (0, 1), (1, 0))]
    fives, sixes = [of(5) for of in angles], [of(6) for of in angles]
    enter = [[pair_of(fives[0], sixes[0], o, i) for i in range(CHUNKS)] for o in range(CHUNKS)]
    before = {(o, i): pair_of(fives[1], sixes[1], o, i) for o, i in EVERY}
    after = {(o, i): pair_of(fives[2], sixes[2], o, i) for o, i in EVERY}
    leave = {(b4, b7): [[None] * CHUNKS for _ in range(CHUNKS)] for b4 in (0, 1) for b7 in (0, 1)}
    for o, i in EVERY:
        terms = [after[o, k] * before[k, i] for k in range(CHUNKS)]
        for (b4, b7), table in leave.items():
            total = None
            for k, term in enumerate(terms):
                term = -term if outer_parity(b4, k >> 1, k & 1, b7) else term
                total = term if total is None else total + term
            table[o][i] = jnp.broadcast_to(total, TILE)
    return gates, enter, leave


def prepare_next(angles_ref, global_ref, gates_ref, spin_ref, sign_ref, last_ref):
    for at, (high, low) in enumerate(section_gates(angles_ref, 1)):
        gates_ref[at, 0] = high
        gates_ref[at, 1] = low
    later = trig(angles_ref, 1, 1)
    half = global_ref[...] * 0.5
    cosines, sines = jnp.cos(half), jnp.sin(half)
    low, high = ((cosines[:, i : i + 1], sines[:, i : i + 1]) for i in (0, 1))
    for o, i in EVERY:
        spin_ref[o, i] = jnp.broadcast_to(pair_of(high, low, o, i), TILE)
        last_ref[o, i] = jnp.broadcast_to(pair_of(later(5), later(6), o, i), TILE)
    edge = edge_tile()
    place5, place6 = lax.axis_index("h3"), lax.axis_index("h0")
    sign5, sign6, both = signs_of(place5), signs_of(place6), signs_of(place5 * place6)
    for b4 in (0, 1):
        for b7 in (0, 1):
            factor = both
            if b4:
                factor = factor * sign5
            if b7:
                factor = factor * sign6
            sign_ref[b4, b7] = edge * factor


def gates_of(gates_ref):
    return [(gates_ref[at, 0], gates_ref[at, 1]) for at in range(4)]


def mixed_chunk(factors, pieces):
    return to_chunk([weighted(factors, [pieces(k, half) for k in range(CHUNKS)]) for half in (0, 1)])


def first_kernel(angles_ref, global_ref, state_ref, out_ref, *refs):
    *next_refs, angles, spins, held, done = refs
    copies = [
        pltpu.make_async_copy(source, target, done.at[at])
        for at, (source, target) in enumerate([(angles_ref, angles), (global_ref, spins), (state_ref, held)])
    ]
    for copy in copies:
        copy.start()
    copies[0].wait()
    gates, enter, leave = prepare_first(angles)
    edge = edge_tile()
    copies[1].wait()
    prepare_next(angles, spins, *next_refs)
    copies[2].wait()
    chunks, signs0 = [], []
    for c in range(CHUNKS):
        chunks.append(mixed_chunk(enter[c], lambda k, half: held[halves(half), k]))
        signs0.append(chunk_sign(lambda b4, b7: -edge if outer_parity(b4, c >> 1, c & 1, b7) else edge))
    chunks = chunk_layers(chunks, gates, signs0, chunk_sign(lambda b4, b7: edge))
    for c, chunk in enumerate(chunks):
        for b0 in (0, 1):
            out_ref[c, halves(b0)] = of_chunk(chunk, b0)
    for (b4, b7), factors in leave.items():
        rows = slice(b7 * 8, b7 * 8 + 8)
        for block in range(b4, BLOCKS, 2):
            tiles = [out_ref[i, block, rows] for i in range(CHUNKS)]
            for o in range(CHUNKS):
                out_ref[o, block, rows] = weighted(factors[o], tiles)


def middle_kernel(gates_ref, spin_ref, sign_ref, in_ref, out_ref):
    factors = [[jnp.concatenate([spin_ref[o, i]] * 2, axis=0)[None] for i in range(CHUNKS)] for o in range(CHUNKS)]
    chunks = [mixed_chunk(factors[c], lambda k, half: in_ref[k, halves(half)]) for c in range(CHUNKS)]
    edge = edge_tile()
    sign0 = chunk_sign(lambda b4, b7: sign_ref[b4, b7])
    chunks = chunk_layers(chunks, gates_of(gates_ref), [sign0] * CHUNKS, chunk_sign(lambda b4, b7: edge))
    for c, chunk in enumerate(chunks):
        for b0 in (0, 1):
            out_ref[c, halves(b0)] = of_chunk(chunk, b0)


def last_kernel(last_ref, in_ref, out_ref, held, done):
    factors = [[last_ref[o, k] for k in range(CHUNKS)] for o in range(CHUNKS)]
    size = BLOCKS // PARTS
    copies = []
    for part in range(PARTS):
        for block in range(part * size, part * size + size):
            for b7 in (0, 1):
                rows = slice(b7 * 8, b7 * 8 + 8)
                tiles = [in_ref[k, block, rows] for k in range(CHUNKS)]
                for o in range(CHUNKS):
                    value = weighted(factors[o], tiles)
                    held[block, o, rows] = -value if outer_parity(block & 1, o >> 1, o & 1, b7) else value
        span = pl.ds(part * size, size)
        copies.append(pltpu.make_async_copy(held.at[span], out_ref.at[span], done.at[part]))
        copies[-1].start()
    for copy in copies:
        copy.wait()


VMEM = pl.BlockSpec(memory_space=pltpu.VMEM)
HBM = pl.BlockSpec(memory_space=pltpu.HBM)
BY_CHUNK = (CHUNKS, BLOCKS, ROWS, LANES)
NATURAL = (BLOCKS, CHUNKS, ROWS, LANES)
CHUNK = (BLOCKS, ROWS, LANES)


def f32(*shape):
    return jax.ShapeDtypeStruct(shape, jnp.float32)


def call(kernel, out_shape, *args, specs=None, out_specs=VMEM, scratch=(), flops=0, limit=16):
    return pl.pallas_call(
        kernel,
        out_shape=out_shape,
        in_specs=specs or [VMEM] * len(args),
        out_specs=out_specs,
        scratch_shapes=scratch,
        cost_estimate=pl.CostEstimate(flops=flops, bytes_accessed=2 * MIB, transcendentals=0),
        compiler_params=pltpu.CompilerParams(vmem_limit_bytes=limit * MIB),
    )(*args)


GATES = jax.ShapeDtypeStruct((4, 2, SIDE, SIDE), jnp.bfloat16)
TABLE = f32(CHUNKS, CHUNKS, *TILE)


def first_call(angles, global_angles, state):
    shapes = (f32(*BY_CHUNK), GATES, TABLE, f32(2, 2, *TILE), TABLE)
    args = [pltpu.with_memory_space_constraint(x, pltpu.HBM) for x in (angles, global_angles, state)]
    return call(
        first_kernel, tuple(pltpu.VMEM(x.shape, x.dtype) for x in shapes), *args, specs=[HBM] * 3, out_specs=(VMEM,) * 5,
        scratch=[
            pltpu.VMEM(angles.shape, jnp.float32),
            pltpu.VMEM(global_angles.shape, jnp.float32),
            pltpu.VMEM(state.shape, jnp.float32),
            pltpu.SemaphoreType.DMA((3,)),
        ],
        flops=1600 * MIB,
    )


def last_call(last, amps):
    return call(
        last_kernel, f32(*NATURAL), last, amps, out_specs=HBM,
        scratch=[pltpu.VMEM(NATURAL, jnp.float32), pltpu.SemaphoreType.DMA((PARTS,))],
    )


def on_device(state, layer_angles, global_angles):
    amps, gates, spin, sign, last = first_call(
        layer_angles.transpose(0, 2, 1, 3), global_angles.reshape(1, 2), state.reshape(NATURAL)
    )
    amps = lax.all_to_all(
        amps.reshape(CHUNKS * BLOCKS, ROWS, LANES), ("h3", "h0", "lo"), split_axis=0, concat_axis=0, tiled=True
    )
    amps = call(middle_kernel, f32(*BY_CHUNK), gates, spin, sign, amps.reshape(BY_CHUNK), flops=1600 * MIB)
    amps = lax.all_to_all(
        amps.reshape(CHUNKS, BLOCKS * ROWS, LANES), ("h3", "h0"), split_axis=0, concat_axis=0, tiled=True
    )
    return last_call(last, amps.reshape(BY_CHUNK)).reshape(state.shape)


def solution(mesh):
    high, low = mesh.shape["hi"], mesh.shape["lo"]
    finer = Mesh(mesh.devices.reshape(2, high // 4, 2, low), ("h3", "hm", "h0", "lo"))
    spec = P(("h3", "hm", "h0"), "lo", None)
    return jax.shard_map(on_device, mesh=finer, in_specs=(spec, P(), P()), out_specs=spec, check_vma=False)
```

```python
import functools

import jax
import jax.numpy as jnp
from jax import lax
from jax.experimental import pallas as pl
from jax.experimental.pallas import tpu as pltpu
from jax.sharding import Mesh
from jax.sharding import PartitionSpec as P

ROW_BITS = (1, 2, 3, 4, 7, 8, 9, 10)
COL_BITS = (0, 11, 12, 13, 14, 15, 16, 17)
SIDE = 256
CHUNKS = 4
BLOCKS = 32
ROWS = 16
LANES = 128
TILE = (8, LANES)
EVERY = [(o, i) for o in range(CHUNKS) for i in range(CHUNKS)]
MIB = 2**20
PARTS = 4


def trig(angles_ref, section, layer):
    half = angles_ref[section, :, layer] * 0.5
    cosines, sines = jnp.cos(half), jnp.sin(half)

    def of(bit):
        group, qubit = bit // 6, bit % 6
        return (
            cosines[group : group + 1, qubit : qubit + 1],
            sines[group : group + 1, qubit : qubit + 1],
        )

    return of


def bit_of(index, place):
    return (index >> place) & 1


def signs_of(parity):
    return (1 - 2 * (parity & 1)).astype(jnp.float32)


def ry(pair, out, inner):
    cosine, sine = pair
    if isinstance(out, int):
        return cosine if out == inner else sine if out == 1 else -sine
    return jnp.where(out == inner, cosine, jnp.where(out == 1, sine, -sine))


def gate(bits, of, transposed):
    row = lax.broadcasted_iota(jnp.int32, TILE, 0)
    lane = lax.broadcasted_iota(jnp.int32, TILE, 1)
    pairs = [(i, i + 1) for i in range(7) if bits[i] + 1 == bits[i + 1]]

    def entry(i, r, c):
        cosine, sine = of(bits[i])
        out, inner = (c, r) if transposed else (r, c)
        if isinstance(c, int):
            return ry((cosine, sine), out, inner)
        return jnp.where(r == c, cosine, jnp.where(out == 1, sine, -sine))

    if transposed:
        out_bit = {i: bit_of(lane, 7 - i) for i in range(1, 8)}
    else:
        out_bit = {i: bit_of(row, 7 - i) for i in range(5, 8)}
    base = jnp.ones(TILE, jnp.float32)
    for i in (5, 6, 7):
        base = base * entry(i, bit_of(row, 7 - i), bit_of(lane, 7 - i))
    parity = jnp.zeros(TILE, jnp.int32)
    for i, j in pairs:
        if i in out_bit and j in out_bit:
            parity = parity + out_bit[i] * out_bit[j]
    tiles = {(): base * signs_of(parity)}
    for i in (4, 3, 2, 1):
        grown = {}
        for r in (0, 1):
            factor = entry(i, r, bit_of(lane, 7 - i))
            if not transposed and r == 1 and (i, i + 1) in pairs and i + 1 in out_bit:
                factor = factor * signs_of(out_bit[i + 1])
            for key, tile in tiles.items():
                grown[(r, *key)] = tile * factor
        tiles = grown
    halves = []
    for c in (0, 1):
        column = {}
        for r in (0, 1):
            factor = entry(0, r, c)
            if transposed and c == 1 and (0, 1) in pairs:
                factor = factor * signs_of(out_bit[1])
            for key, tile in tiles.items():
                column[(r, *key)] = tile * factor
        if not transposed:
            for key in column:
                if sum(key[i] * key[j] for i, j in pairs if j < 5) % 2:
                    column[key] = -column[key]
        halves.append(jnp.concatenate([column[key] for key in sorted(column)], axis=0))
    return jnp.concatenate(halves, axis=1)


def split(value):
    high = value.astype(jnp.bfloat16)
    low = (value - high.astype(jnp.float32)).astype(jnp.bfloat16)
    return high, low


def dot3(left, right):
    mul = functools.partial(jnp.dot, preferred_element_type=jnp.float32)
    return mul(left[0], right[0]) + mul(left[0], right[1]) + mul(left[1], right[0])


def section_gates(angles_ref, section):
    gates = []
    for layer in (0, 1):
        of = trig(angles_ref, section, layer)
        gates.append(split(gate(COL_BITS, of, True)))
        gates.append(split(gate(ROW_BITS, of, False)))
    return gates


def edge_tile():
    row = lax.broadcasted_iota(jnp.int32, TILE, 0)
    lane = lax.broadcasted_iota(jnp.int32, TILE, 1)
    return signs_of(bit_of(row, 0) * bit_of(lane, 6))


def chunk_sign(tile_of):
    tiles = {(b4, b7): tile_of(b4, b7) for b4 in (0, 1) for b7 in (0, 1)}
    columns = []
    for b0 in (0, 1):
        column = []
        for upper in range(16):
            for b7 in (0, 1):
                tile = tiles[upper & 1, b7]
                column.append(-tile if b0 and upper >= 8 else tile)
        columns.append(jnp.concatenate(column, axis=0))
    return jnp.concatenate(columns, axis=1)


def chunk_layers(chunks, gates, signs0, sign1):
    right0, left0, right1, left1 = gates
    chunks = [dot3(split(chunk), right0) for chunk in chunks]
    chunks = [dot3(left0, split(chunk)) * sign for chunk, sign in zip(chunks, signs0, strict=True)]
    chunks = [dot3(split(chunk), right1) for chunk in chunks]
    return [dot3(left1, split(chunk)) * sign1 for chunk in chunks]


def weighted(factors, values):
    total = None
    for factor, value in zip(factors, values, strict=True):
        term = factor * value
        total = term if total is None else total + term
    return total


def to_chunk(pieces):
    return jnp.concatenate([piece.reshape(SIDE, LANES) for piece in pieces], axis=1)


def of_chunk(chunk, half):
    return chunk[:, half * LANES : (half + 1) * LANES].reshape(16, ROWS, LANES)


def halves(half):
    return slice(half * 16, half * 16 + 16)


def rows_of(b7):
    return slice(b7 * 8, b7 * 8 + 8)


def outer_parity(b4, b5, b6, b7):
    return (b4 * b5 + b5 * b6 + b6 * b7) % 2


def pair_of(first, second, out, inner):
    return ry(first, out >> 1, inner >> 1) * ry(second, out & 1, inner & 1)


def prepare_first(angles_ref):
    gates = section_gates(angles_ref, 0)
    angles = [trig(angles_ref, *at) for at in ((0, 0), (0, 1), (1, 0))]
    fives, sixes = [of(5) for of in angles], [of(6) for of in angles]
    enter = [[pair_of(fives[0], sixes[0], o, i) for i in range(CHUNKS)] for o in range(CHUNKS)]
    before = {(o, i): pair_of(fives[1], sixes[1], o, i) for o, i in EVERY}
    after = {(o, i): pair_of(fives[2], sixes[2], o, i) for o, i in EVERY}
    leave = {(b4, b7): [[None] * CHUNKS for _ in range(CHUNKS)] for b4 in (0, 1) for b7 in (0, 1)}
    for o, i in EVERY:
        terms = [after[o, k] * before[k, i] for k in range(CHUNKS)]
        for (b4, b7), table in leave.items():
            total = None
            for k, term in enumerate(terms):
                term = -term if outer_parity(b4, k >> 1, k & 1, b7) else term
                total = term if total is None else total + term
            table[o][i] = jnp.broadcast_to(total, TILE)
    return gates, enter, leave


def prepare_next(angles_ref, global_ref, gates_ref, spin_ref, sign_ref, last_ref):
    for at, (high, low) in enumerate(section_gates(angles_ref, 1)):
        gates_ref[at, 0] = high
        gates_ref[at, 1] = low
    later = trig(angles_ref, 1, 1)
    half = global_ref[...] * 0.5
    cosines, sines = jnp.cos(half), jnp.sin(half)
    low, high = ((cosines[:, i : i + 1], sines[:, i : i + 1]) for i in (0, 1))
    for o, i in EVERY:
        spin_ref[o, i] = jnp.broadcast_to(pair_of(high, low, o, i), TILE)
        last_ref[o, i] = jnp.broadcast_to(pair_of(later(5), later(6), o, i), TILE)
    edge = edge_tile()
    place5, place6 = lax.axis_index("h3"), lax.axis_index("h0")
    sign5, sign6, both = signs_of(place5), signs_of(place6), signs_of(place5 * place6)
    for b4 in (0, 1):
        for b7 in (0, 1):
            factor = both
            if b4:
                factor = factor * sign5
            if b7:
                factor = factor * sign6
            sign_ref[b4, b7] = edge * factor


def gates_of(gates_ref):
    return [(gates_ref[at, 0], gates_ref[at, 1]) for at in range(4)]


def mixed_chunk(factors, pieces):
    return to_chunk([weighted(factors, [pieces(k, half) for k in range(CHUNKS)]) for half in (0, 1)])


def first_kernel(angles_ref, global_ref, state_ref, out_ref, *refs):
    *next_refs, angles, spins, held, done = refs
    copies = [
        pltpu.make_async_copy(source, target, done.at[at])
        for at, (source, target) in enumerate([(angles_ref, angles), (global_ref, spins), (state_ref, held)])
    ]
    for copy in copies:
        copy.start()
    copies[0].wait()
    gates, enter, leave = prepare_first(angles)
    edge = edge_tile()
    copies[1].wait()
    prepare_next(angles, spins, *next_refs)
    copies[2].wait()
    chunks, signs0 = [], []
    for c in range(CHUNKS):
        chunks.append(mixed_chunk(enter[c], lambda k, half: held[halves(half), k]))
        signs0.append(outer_signs(edge, c))
    chunks = chunk_layers(chunks, gates, signs0, chunk_sign(lambda b4, b7: edge))
    for c, chunk in enumerate(chunks):
        for b0 in (0, 1):
            out_ref[c, halves(b0)] = of_chunk(chunk, b0)
    for (b4, b7), factors in leave.items():
        for block in range(b4, BLOCKS, 2):
            tiles = [out_ref[i, block, rows_of(b7)] for i in range(CHUNKS)]
            for o in range(CHUNKS):
                out_ref[o, block, rows_of(b7)] = weighted(factors[o], tiles)


def late():
    return lax.rem(lax.axis_index("lo"), 2) == 1


def outer_signs(edge, c):
    return chunk_sign(lambda b4, b7: -edge if outer_parity(b4, c >> 1, c & 1, b7) else edge)


def middle_kernel(gates_ref, spin_ref, sign_ref, in_ref, out_ref):
    @pl.when(late())
    def _():
        factors = [[spin_ref[o, i] for i in range(CHUNKS)] for o in range(CHUNKS)]
        for block in range(BLOCKS):
            for b7 in (0, 1):
                tiles = [in_ref[i, block, rows_of(b7)] for i in range(CHUNKS)]
                for o in range(CHUNKS):
                    out_ref[o, block, rows_of(b7)] = weighted(factors[o], tiles)

    @pl.when(jnp.logical_not(late()))
    def _():
        factors = [[jnp.concatenate([spin_ref[o, i]] * 2, axis=0)[None] for i in range(CHUNKS)] for o in range(CHUNKS)]
        chunks = [mixed_chunk(factors[c], lambda k, half: in_ref[k, halves(half)]) for c in range(CHUNKS)]
        edge = edge_tile()
        sign0 = chunk_sign(lambda b4, b7: sign_ref[b4, b7])
        chunks = chunk_layers(chunks, gates_of(gates_ref), [sign0] * CHUNKS, chunk_sign(lambda b4, b7: edge))
        for c, chunk in enumerate(chunks):
            for b0 in (0, 1):
                out_ref[c, halves(b0)] = of_chunk(chunk, b0)


def last_kernel(gates_ref, last_ref, in_ref, out_ref, held, done):
    @pl.when(late())
    def _():
        right0, left0, right1, left1 = gates_of(gates_ref)
        edge = edge_tile()
        chunks = [to_chunk([in_ref[c, halves(b0)] for b0 in (0, 1)]) for c in range(CHUNKS)]
        chunks = [dot3(split(chunk), right0) for chunk in chunks]
        chunks = [dot3(left0, split(chunk)) * outer_signs(edge, c) for c, chunk in enumerate(chunks)]
        factors = [[last_ref[o, i][0:1, 0:1] for i in range(CHUNKS)] for o in range(CHUNKS)]
        chunks = [weighted(factors[o], chunks) for o in range(CHUNKS)]
        chunks = [dot3(split(chunk), right1) for chunk in chunks]
        copies = []
        for c, chunk in enumerate(chunks):
            chunk = dot3(left1, split(chunk)) * outer_signs(edge, c)
            for b0 in (0, 1):
                held[halves(b0), c] = of_chunk(chunk, b0)
            copies.append(pltpu.make_async_copy(held.at[:, c], out_ref.at[:, c], done.at[c]))
            copies[-1].start()
        for copy in copies:
            copy.wait()

    @pl.when(jnp.logical_not(late()))
    def _():
        factors = [[last_ref[o, i] for i in range(CHUNKS)] for o in range(CHUNKS)]
        size = BLOCKS // PARTS
        copies = []
        for part in range(PARTS):
            for block in range(part * size, part * size + size):
                for b7 in (0, 1):
                    tiles = [in_ref[i, block, rows_of(b7)] for i in range(CHUNKS)]
                    for o in range(CHUNKS):
                        value = weighted(factors[o], tiles)
                        value = -value if outer_parity(block & 1, o >> 1, o & 1, b7) else value
                        held[block, o, rows_of(b7)] = value
            span = pl.ds(part * size, size)
            copies.append(pltpu.make_async_copy(held.at[span], out_ref.at[span], done.at[part]))
            copies[-1].start()
        for copy in copies:
            copy.wait()


VMEM = pl.BlockSpec(memory_space=pltpu.VMEM)
HBM = pl.BlockSpec(memory_space=pltpu.HBM)
BY_CHUNK = (CHUNKS, BLOCKS, ROWS, LANES)
NATURAL = (BLOCKS, CHUNKS, ROWS, LANES)
CHUNK = (BLOCKS, ROWS, LANES)


def f32(*shape):
    return jax.ShapeDtypeStruct(shape, jnp.float32)


def call(kernel, out_shape, *args, specs=None, out_specs=VMEM, scratch=(), flops=0, limit=16):
    return pl.pallas_call(
        kernel,
        out_shape=out_shape,
        in_specs=specs or [VMEM] * len(args),
        out_specs=out_specs,
        scratch_shapes=scratch,
        cost_estimate=pl.CostEstimate(flops=flops, bytes_accessed=2 * MIB, transcendentals=0),
        compiler_params=pltpu.CompilerParams(vmem_limit_bytes=limit * MIB),
    )(*args)


GATES = jax.ShapeDtypeStruct((4, 2, SIDE, SIDE), jnp.bfloat16)
TABLE = f32(CHUNKS, CHUNKS, *TILE)


def first_call(angles, global_angles, state):
    shapes = (f32(*BY_CHUNK), GATES, TABLE, f32(2, 2, *TILE), TABLE)
    args = [pltpu.with_memory_space_constraint(x, pltpu.HBM) for x in (angles, global_angles, state)]
    return call(
        first_kernel, tuple(pltpu.VMEM(x.shape, x.dtype) for x in shapes), *args, specs=[HBM] * 3, out_specs=(VMEM,) * 5,
        scratch=[
            pltpu.VMEM(angles.shape, jnp.float32),
            pltpu.VMEM(global_angles.shape, jnp.float32),
            pltpu.VMEM(state.shape, jnp.float32),
            pltpu.SemaphoreType.DMA((3,)),
        ],
        flops=1600 * MIB,
    )


def last_call(gates, last, amps):
    return call(
        last_kernel, f32(*NATURAL), gates, last, amps, out_specs=HBM,
        scratch=[pltpu.VMEM(NATURAL, jnp.float32), pltpu.SemaphoreType.DMA((PARTS,))],
    )


def on_device(state, layer_angles, global_angles):
    amps, gates, spin, sign, last = first_call(
        layer_angles.transpose(0, 2, 1, 3), global_angles.reshape(1, 2), state.reshape(NATURAL)
    )
    amps = lax.all_to_all(
        amps.reshape(CHUNKS * BLOCKS, ROWS, LANES), ("h3", "h0", "lo"), split_axis=0, concat_axis=0, tiled=True
    )
    amps = call(middle_kernel, f32(*BY_CHUNK), gates, spin, sign, amps.reshape(BY_CHUNK), flops=1600 * MIB)
    amps = lax.all_to_all(
        amps.reshape(CHUNKS, BLOCKS * ROWS, LANES), ("h3", "h0"), split_axis=0, concat_axis=0, tiled=True
    )
    return last_call(gates, last, amps.reshape(BY_CHUNK)).reshape(state.shape)


def solution(mesh):
    high, low = mesh.shape["hi"], mesh.shape["lo"]
    finer = Mesh(mesh.devices.reshape(2, high // 4, 2, low), ("h3", "hm", "h0", "lo"))
    spec = P(("h3", "hm", "h0"), "lo", None)
    return jax.shard_map(on_device, mesh=finer, in_specs=(spec, P(), P()), out_specs=spec, check_vma=False)
```

```python
import functools

import jax
import jax.numpy as jnp
from jax import lax
from jax.experimental import pallas as pl
from jax.experimental.pallas import tpu as pltpu
from jax.sharding import Mesh
from jax.sharding import PartitionSpec as P

ROW_BITS = (1, 2, 3, 4, 7, 8, 9, 10)
COL_BITS = (0, 11, 12, 13, 14, 15, 16, 17)
SIDE = 256
CHUNKS = 4
BLOCKS = 32
ROWS = 16
LANES = 128
TILE = (8, LANES)
EVERY = [(o, i) for o in range(CHUNKS) for i in range(CHUNKS)]
MIB = 2**20
PARTS = 4


def trig(angles_ref, section, layer):
    half = angles_ref[section, :, layer] * 0.5
    cosines, sines = jnp.cos(half), jnp.sin(half)

    def of(bit):
        group, qubit = bit // 6, bit % 6
        return (
            cosines[group : group + 1, qubit : qubit + 1],
            sines[group : group + 1, qubit : qubit + 1],
        )

    return of


def bit_of(index, place):
    return (index >> place) & 1


def signs_of(parity):
    return (1 - 2 * (parity & 1)).astype(jnp.float32)


def ry(pair, out, inner):
    cosine, sine = pair
    if isinstance(out, int):
        return cosine if out == inner else sine if out == 1 else -sine
    return jnp.where(out == inner, cosine, jnp.where(out == 1, sine, -sine))


def gate(bits, of, transposed):
    row = lax.broadcasted_iota(jnp.int32, TILE, 0)
    lane = lax.broadcasted_iota(jnp.int32, TILE, 1)
    pairs = [(i, i + 1) for i in range(7) if bits[i] + 1 == bits[i + 1]]

    def entry(i, r, c):
        cosine, sine = of(bits[i])
        out, inner = (c, r) if transposed else (r, c)
        if isinstance(c, int):
            return ry((cosine, sine), out, inner)
        return jnp.where(r == c, cosine, jnp.where(out == 1, sine, -sine))

    if transposed:
        out_bit = {i: bit_of(lane, 7 - i) for i in range(1, 8)}
    else:
        out_bit = {i: bit_of(row, 7 - i) for i in range(5, 8)}
    base = jnp.ones(TILE, jnp.float32)
    for i in (5, 6, 7):
        base = base * entry(i, bit_of(row, 7 - i), bit_of(lane, 7 - i))
    parity = jnp.zeros(TILE, jnp.int32)
    for i, j in pairs:
        if i in out_bit and j in out_bit:
            parity = parity + out_bit[i] * out_bit[j]
    tiles = {(): base * signs_of(parity)}
    for i in (4, 3, 2, 1):
        grown = {}
        for r in (0, 1):
            factor = entry(i, r, bit_of(lane, 7 - i))
            if not transposed and r == 1 and (i, i + 1) in pairs and i + 1 in out_bit:
                factor = factor * signs_of(out_bit[i + 1])
            for key, tile in tiles.items():
                grown[(r, *key)] = tile * factor
        tiles = grown
    halves = []
    for c in (0, 1):
        column = {}
        for r in (0, 1):
            factor = entry(0, r, c)
            if transposed and c == 1 and (0, 1) in pairs:
                factor = factor * signs_of(out_bit[1])
            for key, tile in tiles.items():
                column[(r, *key)] = tile * factor
        if not transposed:
            for key in column:
                if sum(key[i] * key[j] for i, j in pairs if j < 5) % 2:
                    column[key] = -column[key]
        halves.append(jnp.concatenate([column[key] for key in sorted(column)], axis=0))
    return jnp.concatenate(halves, axis=1)


def split(value):
    high = value.astype(jnp.bfloat16)
    low = (value - high.astype(jnp.float32)).astype(jnp.bfloat16)
    return high, low


def dot3(left, right):
    mul = functools.partial(jnp.dot, preferred_element_type=jnp.float32)
    return mul(left[0], right[0]) + mul(left[0], right[1]) + mul(left[1], right[0])


def section_gates(angles_ref, section):
    gates = []
    for layer in (0, 1):
        of = trig(angles_ref, section, layer)
        gates.append(split(gate(COL_BITS, of, True)))
        gates.append(split(gate(ROW_BITS, of, False)))
    return gates


def edge_tile():
    row = lax.broadcasted_iota(jnp.int32, TILE, 0)
    lane = lax.broadcasted_iota(jnp.int32, TILE, 1)
    return signs_of(bit_of(row, 0) * bit_of(lane, 6))


def chunk_sign(tile_of):
    tiles = {(b4, b7): tile_of(b4, b7) for b4 in (0, 1) for b7 in (0, 1)}
    columns = []
    for b0 in (0, 1):
        column = []
        for upper in range(16):
            for b7 in (0, 1):
                tile = tiles[upper & 1, b7]
                column.append(-tile if b0 and upper >= 8 else tile)
        columns.append(jnp.concatenate(column, axis=0))
    return jnp.concatenate(columns, axis=1)


def chunk_layers(chunks, gates, signs0, sign1):
    right0, left0, right1, left1 = gates
    chunks = [dot3(split(chunk), right0) for chunk in chunks]
    chunks = [dot3(left0, split(chunk)) * sign for chunk, sign in zip(chunks, signs0, strict=True)]
    chunks = [dot3(split(chunk), right1) for chunk in chunks]
    return [dot3(left1, split(chunk)) * sign1 for chunk in chunks]


def weighted(factors, values):
    total = None
    for factor, value in zip(factors, values, strict=True):
        term = factor * value
        total = term if total is None else total + term
    return total


def to_chunk(pieces):
    return jnp.concatenate([piece.reshape(SIDE, LANES) for piece in pieces], axis=1)


def of_chunk(chunk, half):
    return chunk[:, half * LANES : (half + 1) * LANES].reshape(16, ROWS, LANES)


def halves(half):
    return slice(half * 16, half * 16 + 16)


def spot(c, block):
    z, x, core = block // 8, block // 2 % 4, block % 2
    return (((c % 2) * 4 + x) * 2 + core) * 8 + (c // 2) * 4 + z


def rows_of(b7):
    return slice(b7 * 8, b7 * 8 + 8)


def outer_parity(b4, b5, b6, b7):
    return (b4 * b5 + b5 * b6 + b6 * b7) % 2


def pair_of(first, second, out, inner):
    return ry(first, out >> 1, inner >> 1) * ry(second, out & 1, inner & 1)


def prepare_first(angles_ref):
    gates = section_gates(angles_ref, 0)
    angles = [trig(angles_ref, *at) for at in ((0, 0), (0, 1), (1, 0))]
    fives, sixes = [of(5) for of in angles], [of(6) for of in angles]
    enter = [[pair_of(fives[0], sixes[0], o, i) for i in range(CHUNKS)] for o in range(CHUNKS)]
    before = {(o, i): pair_of(fives[1], sixes[1], o, i) for o, i in EVERY}
    after = {(o, i): pair_of(fives[2], sixes[2], o, i) for o, i in EVERY}
    leave = {(b4, b7): [[None] * CHUNKS for _ in range(CHUNKS)] for b4 in (0, 1) for b7 in (0, 1)}
    for o, i in EVERY:
        terms = [after[o, k] * before[k, i] for k in range(CHUNKS)]
        for (b4, b7), table in leave.items():
            total = None
            for k, term in enumerate(terms):
                term = -term if outer_parity(b4, k >> 1, k & 1, b7) else term
                total = term if total is None else total + term
            table[o][i] = jnp.broadcast_to(total, TILE)
    return gates, enter, leave


def prepare_next(angles_ref, global_ref, kept_ref, spin_ref, sign_ref, last_ref):
    kept_ref[...] = angles_ref[...]
    later = trig(angles_ref, 1, 1)
    half = global_ref[...] * 0.5
    cosines, sines = jnp.cos(half), jnp.sin(half)
    low, high = ((cosines[:, i : i + 1], sines[:, i : i + 1]) for i in (0, 1))
    for o, i in EVERY:
        spin_ref[o, i] = jnp.broadcast_to(pair_of(high, low, o, i), TILE)
        last_ref[o, i] = jnp.broadcast_to(pair_of(later(5), later(6), o, i), TILE)
    edge = edge_tile()
    place5, place6 = lax.axis_index("h3"), lax.axis_index("h0")
    sign5, sign6, both = signs_of(place5), signs_of(place6), signs_of(place5 * place6)
    for b4 in (0, 1):
        for b7 in (0, 1):
            factor = both
            if b4:
                factor = factor * sign5
            if b7:
                factor = factor * sign6
            sign_ref[b4, b7] = edge * factor


def mixed_chunk(factors, pieces):
    return to_chunk([weighted(factors, [pieces(k, half) for k in range(CHUNKS)]) for half in (0, 1)])


def first_kernel(angles_ref, global_ref, state_ref, out_ref, *refs):
    *next_refs, angles, spins, held, done = refs
    copies = [
        pltpu.make_async_copy(source, target, done.at[at])
        for at, (source, target) in enumerate([(angles_ref, angles), (global_ref, spins), (state_ref, held)])
    ]
    for copy in copies:
        copy.start()
    copies[0].wait()
    gates, enter, leave = prepare_first(angles)
    edge = edge_tile()
    copies[1].wait()
    prepare_next(angles, spins, *next_refs)
    copies[2].wait()
    chunks, signs0 = [], []
    for c in range(CHUNKS):
        chunks.append(mixed_chunk(enter[c], lambda k, half: held[halves(half), k]))
        signs0.append(outer_signs(edge, c))
    chunks = chunk_layers(chunks, gates, signs0, chunk_sign(lambda b4, b7: edge))
    for c, chunk in enumerate(chunks):
        for b0 in (0, 1):
            piece = of_chunk(chunk, b0)
            for at in range(16):
                out_ref[spot(c, b0 * 16 + at)] = piece[at]
    for (b4, b7), factors in leave.items():
        for block in range(b4, BLOCKS, 2):
            tiles = [out_ref[spot(i, block), rows_of(b7)] for i in range(CHUNKS)]
            for o in range(CHUNKS):
                out_ref[spot(o, block), rows_of(b7)] = weighted(factors[o], tiles)


def late():
    return lax.axis_index("core") == 1


def outer_signs(edge, c):
    return chunk_sign(lambda b4, b7: -edge if outer_parity(b4, c >> 1, c & 1, b7) else edge)


def middle_kernel(angles_ref, spin_ref, sign_ref, in_ref, out_ref):
    @pl.when(late())
    def _():
        factors = [[spin_ref[o, i] for i in range(CHUNKS)] for o in range(CHUNKS)]
        for block in range(BLOCKS):
            for b7 in (0, 1):
                tiles = [in_ref[spot(i, block), rows_of(b7)] for i in range(CHUNKS)]
                for o in range(CHUNKS):
                    out_ref[o, block, rows_of(b7)] = weighted(factors[o], tiles)

    @pl.when(jnp.logical_not(late()))
    def _():
        def half_of(k, half):
            return jnp.stack([in_ref[spot(k, half * 16 + at)] for at in range(16)])

        factors = [[jnp.concatenate([spin_ref[o, i]] * 2, axis=0)[None] for i in range(CHUNKS)] for o in range(CHUNKS)]
        chunks = [mixed_chunk(factors[c], half_of) for c in range(CHUNKS)]
        edge = edge_tile()
        sign0 = chunk_sign(lambda b4, b7: sign_ref[b4, b7])
        chunks = chunk_layers(chunks, section_gates(angles_ref, 1), [sign0] * CHUNKS, chunk_sign(lambda b4, b7: edge))
        for c, chunk in enumerate(chunks):
            for b0 in (0, 1):
                out_ref[c, halves(b0)] = of_chunk(chunk, b0)


def last_kernel(angles_ref, last_ref, in_ref, out_ref, held, done):
    @pl.when(late())
    def _():
        right0, left0, right1, left1 = section_gates(angles_ref, 1)
        edge = edge_tile()
        chunks = [to_chunk([in_ref[c, halves(b0)] for b0 in (0, 1)]) for c in range(CHUNKS)]
        chunks = [dot3(split(chunk), right0) for chunk in chunks]
        chunks = [dot3(left0, split(chunk)) * outer_signs(edge, c) for c, chunk in enumerate(chunks)]
        factors = [[last_ref[o, i][0:1, 0:1] for i in range(CHUNKS)] for o in range(CHUNKS)]
        chunks = [weighted(factors[o], chunks) for o in range(CHUNKS)]
        chunks = [dot3(split(chunk), right1) for chunk in chunks]
        copies = []
        for c, chunk in enumerate(chunks):
            chunk = dot3(left1, split(chunk)) * outer_signs(edge, c)
            for b0 in (0, 1):
                held[halves(b0), c] = of_chunk(chunk, b0)
            copies.append(pltpu.make_async_copy(held.at[:, c], out_ref.at[:, c], done.at[c]))
            copies[-1].start()
        for copy in copies:
            copy.wait()

    @pl.when(jnp.logical_not(late()))
    def _():
        factors = [[last_ref[o, i] for i in range(CHUNKS)] for o in range(CHUNKS)]
        size = BLOCKS // PARTS
        copies = []
        for part in range(PARTS):
            for block in range(part * size, part * size + size):
                for b7 in (0, 1):
                    tiles = [in_ref[i, block, rows_of(b7)] for i in range(CHUNKS)]
                    for o in range(CHUNKS):
                        value = weighted(factors[o], tiles)
                        value = -value if outer_parity(block & 1, o >> 1, o & 1, b7) else value
                        held[block, o, rows_of(b7)] = value
            span = pl.ds(part * size, size)
            copies.append(pltpu.make_async_copy(held.at[span], out_ref.at[span], done.at[part]))
            copies[-1].start()
        for copy in copies:
            copy.wait()


VMEM = pl.BlockSpec(memory_space=pltpu.VMEM)
HBM = pl.BlockSpec(memory_space=pltpu.HBM)
BY_CHUNK = (CHUNKS, BLOCKS, ROWS, LANES)
NATURAL = (BLOCKS, CHUNKS, ROWS, LANES)
CHUNK = (BLOCKS, ROWS, LANES)


BY_SPOT = (CHUNKS * BLOCKS, ROWS, LANES)
GROUP = ("h0", "x", "core", "h3", "z")


def f32(*shape):
    return jax.ShapeDtypeStruct(shape, jnp.float32)


def call(kernel, out_shape, *args, specs=None, out_specs=VMEM, scratch=(), flops=0, limit=16):
    return pl.pallas_call(
        kernel,
        out_shape=out_shape,
        in_specs=specs or [VMEM] * len(args),
        out_specs=out_specs,
        scratch_shapes=scratch,
        cost_estimate=pl.CostEstimate(flops=flops, bytes_accessed=2 * MIB, transcendentals=0),
        compiler_params=pltpu.CompilerParams(vmem_limit_bytes=limit * MIB),
    )(*args)


TABLE = f32(CHUNKS, CHUNKS, *TILE)


def first_call(angles, global_angles, state):
    shapes = (f32(*BY_SPOT), f32(*angles.shape), TABLE, f32(2, 2, *TILE), TABLE)
    args = [pltpu.with_memory_space_constraint(x, pltpu.HBM) for x in (angles, global_angles, state)]
    return call(
        first_kernel, tuple(pltpu.VMEM(x.shape, x.dtype) for x in shapes), *args, specs=[HBM] * 3, out_specs=(VMEM,) * 5,
        scratch=[
            pltpu.VMEM(angles.shape, jnp.float32),
            pltpu.VMEM(global_angles.shape, jnp.float32),
            pltpu.VMEM(state.shape, jnp.float32),
            pltpu.SemaphoreType.DMA((3,)),
        ],
        flops=1600 * MIB,
    )


def last_call(angles, last, amps):
    return call(
        last_kernel, f32(*NATURAL), angles, last, amps, out_specs=HBM,
        scratch=[pltpu.VMEM(NATURAL, jnp.float32), pltpu.SemaphoreType.DMA((PARTS,))],
    )


def on_device(state, layer_angles, global_angles):
    amps, angles, spin, sign, last = first_call(
        layer_angles.transpose(0, 2, 1, 3), global_angles.reshape(1, 2), state.reshape(NATURAL)
    )
    amps = lax.all_to_all(amps, GROUP, split_axis=0, concat_axis=0, tiled=True)
    amps = call(middle_kernel, f32(*BY_CHUNK), angles, spin, sign, amps, flops=1600 * MIB)
    amps = lax.all_to_all(
        amps.reshape(CHUNKS, BLOCKS * ROWS, LANES), ("h3", "h0"), split_axis=0, concat_axis=0, tiled=True
    )
    return last_call(angles, last, amps.reshape(BY_CHUNK)).reshape(state.shape)


def solution(mesh):
    high, low = mesh.shape["hi"], mesh.shape["lo"]
    sizes = (2, high // 4, 2, 4, low // 8, 2)
    finer = Mesh(mesh.devices.reshape(sizes), ("h3", "hm", "h0", "z", "x", "core"))
    spec = P(("h3", "hm", "h0"), ("z", "x", "core"), None)
    return jax.shard_map(on_device, mesh=finer, in_specs=(spec, P(), P()), out_specs=spec, check_vma=False)
```

```python
import functools

import jax
import jax.numpy as jnp
from jax import lax
from jax.experimental import pallas as pl
from jax.experimental.pallas import tpu as pltpu
from jax.sharding import Mesh
from jax.sharding import PartitionSpec as P

ROW_BITS = (1, 2, 3, 4, 7, 8, 9, 10)
COL_BITS = (0, 11, 12, 13, 14, 15, 16, 17)
SIDE = 256
CHUNKS = 4
BLOCKS = 32
ROWS = 16
LANES = 128
TILE = (8, LANES)
EVERY = [(o, i) for o in range(CHUNKS) for i in range(CHUNKS)]
MIB = 2**20
PARTS = 4


def trig(angles_ref, section, layer):
    half = angles_ref[section, :, layer] * 0.5
    cosines, sines = jnp.cos(half), jnp.sin(half)

    def of(bit):
        group, qubit = bit // 6, bit % 6
        return (
            cosines[group : group + 1, qubit : qubit + 1],
            sines[group : group + 1, qubit : qubit + 1],
        )

    return of


def bit_of(index, place):
    return (index >> place) & 1


def signs_of(parity):
    return (1 - 2 * (parity & 1)).astype(jnp.float32)


def ry(pair, out, inner):
    cosine, sine = pair
    if isinstance(out, int):
        return cosine if out == inner else sine if out == 1 else -sine
    return jnp.where(out == inner, cosine, jnp.where(out == 1, sine, -sine))


def gate(bits, of, transposed):
    row = lax.broadcasted_iota(jnp.int32, TILE, 0)
    lane = lax.broadcasted_iota(jnp.int32, TILE, 1)
    pairs = [(i, i + 1) for i in range(7) if bits[i] + 1 == bits[i + 1]]

    def entry(i, r, c):
        cosine, sine = of(bits[i])
        out, inner = (c, r) if transposed else (r, c)
        if isinstance(c, int):
            return ry((cosine, sine), out, inner)
        return jnp.where(r == c, cosine, jnp.where(out == 1, sine, -sine))

    if transposed:
        out_bit = {i: bit_of(lane, 7 - i) for i in range(1, 8)}
    else:
        out_bit = {i: bit_of(row, 7 - i) for i in range(5, 8)}
    base = jnp.ones(TILE, jnp.float32)
    for i in (5, 6, 7):
        base = base * entry(i, bit_of(row, 7 - i), bit_of(lane, 7 - i))
    parity = jnp.zeros(TILE, jnp.int32)
    for i, j in pairs:
        if i in out_bit and j in out_bit:
            parity = parity + out_bit[i] * out_bit[j]
    tiles = {(): base * signs_of(parity)}
    for i in (4, 3, 2, 1):
        grown = {}
        for r in (0, 1):
            factor = entry(i, r, bit_of(lane, 7 - i))
            if not transposed and r == 1 and (i, i + 1) in pairs and i + 1 in out_bit:
                factor = factor * signs_of(out_bit[i + 1])
            for key, tile in tiles.items():
                grown[(r, *key)] = tile * factor
        tiles = grown
    halves = []
    for c in (0, 1):
        column = {}
        for r in (0, 1):
            factor = entry(0, r, c)
            if transposed and c == 1 and (0, 1) in pairs:
                factor = factor * signs_of(out_bit[1])
            for key, tile in tiles.items():
                column[(r, *key)] = tile * factor
        if not transposed:
            for key in column:
                if sum(key[i] * key[j] for i, j in pairs if j < 5) % 2:
                    column[key] = -column[key]
        halves.append(jnp.concatenate([column[key] for key in sorted(column)], axis=0))
    return jnp.concatenate(halves, axis=1)


def split(value):
    high = value.astype(jnp.bfloat16)
    low = (value - high.astype(jnp.float32)).astype(jnp.bfloat16)
    return high, low


def dot3(left, right):
    mul = functools.partial(jnp.dot, preferred_element_type=jnp.float32)
    return mul(left[0], right[0]) + mul(left[0], right[1]) + mul(left[1], right[0])


def section_gates(angles_ref, section):
    gates = []
    for layer in (0, 1):
        of = trig(angles_ref, section, layer)
        gates.append(split(gate(COL_BITS, of, True)))
        gates.append(split(gate(ROW_BITS, of, False)))
    return gates


def edge_tile():
    row = lax.broadcasted_iota(jnp.int32, TILE, 0)
    lane = lax.broadcasted_iota(jnp.int32, TILE, 1)
    return signs_of(bit_of(row, 0) * bit_of(lane, 6))


def chunk_sign(tile_of):
    tiles = {(b4, b7): tile_of(b4, b7) for b4 in (0, 1) for b7 in (0, 1)}
    columns = []
    for b0 in (0, 1):
        column = []
        for upper in range(16):
            for b7 in (0, 1):
                tile = tiles[upper & 1, b7]
                column.append(-tile if b0 and upper >= 8 else tile)
        columns.append(jnp.concatenate(column, axis=0))
    return jnp.concatenate(columns, axis=1)


def chunk_layers(chunks, gates, signs0, sign1):
    right0, left0, right1, left1 = gates
    chunks = [dot3(split(chunk), right0) for chunk in chunks]
    chunks = [dot3(left0, split(chunk)) * sign for chunk, sign in zip(chunks, signs0, strict=True)]
    chunks = [dot3(split(chunk), right1) for chunk in chunks]
    return [dot3(left1, split(chunk)) * sign1 for chunk in chunks]


def weighted(factors, values):
    total = None
    for factor, value in zip(factors, values, strict=True):
        term = factor * value
        total = term if total is None else total + term
    return total


def to_chunk(pieces):
    return jnp.concatenate([piece.reshape(SIDE, LANES) for piece in pieces], axis=1)


def of_chunk(chunk, half):
    return chunk[:, half * LANES : (half + 1) * LANES].reshape(16, ROWS, LANES)


def halves(half):
    return slice(half * 16, half * 16 + 16)


def spot(c, block):
    z, x, core = block // 8, block // 2 % 4, block % 2
    return (((c % 2) * 4 + x) * 2 + core) * 8 + (c // 2) * 4 + z


def seat(c):
    return c % 2 * 2 + c // 2


def rows_of(b7):
    return slice(b7 * 8, b7 * 8 + 8)


def outer_parity(b4, b5, b6, b7):
    return (b4 * b5 + b5 * b6 + b6 * b7) % 2


def pair_of(first, second, out, inner):
    return ry(first, out >> 1, inner >> 1) * ry(second, out & 1, inner & 1)


def prepare_first(angles_ref):
    gates = section_gates(angles_ref, 0)
    angles = [trig(angles_ref, *at) for at in ((0, 0), (0, 1), (1, 0))]
    fives, sixes = [of(5) for of in angles], [of(6) for of in angles]
    enter = [[pair_of(fives[0], sixes[0], o, i) for i in range(CHUNKS)] for o in range(CHUNKS)]
    before = {(o, i): pair_of(fives[1], sixes[1], o, i) for o, i in EVERY}
    after = {(o, i): pair_of(fives[2], sixes[2], o, i) for o, i in EVERY}
    leave = {(b4, b7): [[None] * CHUNKS for _ in range(CHUNKS)] for b4 in (0, 1) for b7 in (0, 1)}
    for o, i in EVERY:
        terms = [after[o, k] * before[k, i] for k in range(CHUNKS)]
        for (b4, b7), table in leave.items():
            total = None
            for k, term in enumerate(terms):
                term = -term if outer_parity(b4, k >> 1, k & 1, b7) else term
                total = term if total is None else total + term
            table[o][i] = jnp.broadcast_to(total, TILE)
    return gates, enter, leave


def prepare_next(angles_ref, global_ref, kept_ref, spin_ref, sign_ref, last_ref):
    kept_ref[...] = angles_ref[...]
    later = trig(angles_ref, 1, 1)
    half = global_ref[...] * 0.5
    cosines, sines = jnp.cos(half), jnp.sin(half)
    low, high = ((cosines[:, i : i + 1], sines[:, i : i + 1]) for i in (0, 1))
    for o, i in EVERY:
        spin_ref[o, i] = jnp.broadcast_to(pair_of(high, low, o, i), TILE)
        last_ref[o, i] = jnp.broadcast_to(pair_of(later(5), later(6), o, i), TILE)
    edge = edge_tile()
    place5, place6 = lax.axis_index("h3"), lax.axis_index("h0")
    sign5, sign6, both = signs_of(place5), signs_of(place6), signs_of(place5 * place6)
    for b4 in (0, 1):
        for b7 in (0, 1):
            factor = both
            if b4:
                factor = factor * sign5
            if b7:
                factor = factor * sign6
            sign_ref[b4, b7] = edge * factor


def mixed_chunk(factors, pieces):
    return to_chunk([weighted(factors, [pieces(k, half) for k in range(CHUNKS)]) for half in (0, 1)])


def first_kernel(angles_ref, global_ref, state_ref, out_ref, *refs):
    *next_refs, angles, spins, held, done = refs
    copies = [
        pltpu.make_async_copy(source, target, done.at[at])
        for at, (source, target) in enumerate([(angles_ref, angles), (global_ref, spins), (state_ref, held)])
    ]
    for copy in copies:
        copy.start()
    copies[0].wait()
    gates, enter, leave = prepare_first(angles)
    edge = edge_tile()
    copies[1].wait()
    prepare_next(angles, spins, *next_refs)
    copies[2].wait()
    chunks, signs0 = [], []
    for c in range(CHUNKS):
        chunks.append(mixed_chunk(enter[c], lambda k, half: held[halves(half), k]))
        signs0.append(outer_signs(edge, c))
    chunks = chunk_layers(chunks, gates, signs0, chunk_sign(lambda b4, b7: edge))
    for c, chunk in enumerate(chunks):
        for b0 in (0, 1):
            piece = of_chunk(chunk, b0)
            for at in range(16):
                out_ref[spot(c, b0 * 16 + at)] = piece[at]
    for (b4, b7), factors in leave.items():
        for block in range(b4, BLOCKS, 2):
            tiles = [out_ref[spot(i, block), rows_of(b7)] for i in range(CHUNKS)]
            for o in range(CHUNKS):
                out_ref[spot(o, block), rows_of(b7)] = weighted(factors[o], tiles)


def late():
    return lax.axis_index("core") == 1


def outer_signs(edge, c):
    return chunk_sign(lambda b4, b7: -edge if outer_parity(b4, c >> 1, c & 1, b7) else edge)


def middle_kernel(angles_ref, spin_ref, sign_ref, in_ref, out_ref):
    @pl.when(late())
    def _():
        factors = [[spin_ref[o, i] for i in range(CHUNKS)] for o in range(CHUNKS)]
        for block in range(BLOCKS):
            for b7 in (0, 1):
                tiles = [in_ref[spot(i, block), rows_of(b7)] for i in range(CHUNKS)]
                for o in range(CHUNKS):
                    out_ref[seat(o), block, rows_of(b7)] = weighted(factors[o], tiles)

    @pl.when(jnp.logical_not(late()))
    def _():
        def half_of(k, half):
            return jnp.stack([in_ref[spot(k, half * 16 + at)] for at in range(16)])

        factors = [[jnp.concatenate([spin_ref[o, i]] * 2, axis=0)[None] for i in range(CHUNKS)] for o in range(CHUNKS)]
        chunks = [mixed_chunk(factors[c], half_of) for c in range(CHUNKS)]
        edge = edge_tile()
        sign0 = chunk_sign(lambda b4, b7: sign_ref[b4, b7])
        chunks = chunk_layers(chunks, section_gates(angles_ref, 1), [sign0] * CHUNKS, chunk_sign(lambda b4, b7: edge))
        for c, chunk in enumerate(chunks):
            for b0 in (0, 1):
                out_ref[seat(c), halves(b0)] = of_chunk(chunk, b0)


def last_kernel(angles_ref, last_ref, in_ref, out_ref, held, done):
    @pl.when(late())
    def _():
        right0, left0, right1, left1 = section_gates(angles_ref, 1)
        edge = edge_tile()
        chunks = [to_chunk([in_ref[seat(c), halves(b0)] for b0 in (0, 1)]) for c in range(CHUNKS)]
        chunks = [dot3(split(chunk), right0) for chunk in chunks]
        chunks = [dot3(left0, split(chunk)) * outer_signs(edge, c) for c, chunk in enumerate(chunks)]
        factors = [[last_ref[o, i][0:1, 0:1] for i in range(CHUNKS)] for o in range(CHUNKS)]
        chunks = [weighted(factors[o], chunks) for o in range(CHUNKS)]
        chunks = [dot3(split(chunk), right1) for chunk in chunks]
        copies = []
        for c, chunk in enumerate(chunks):
            chunk = dot3(left1, split(chunk)) * outer_signs(edge, c)
            for b0 in (0, 1):
                held[halves(b0), c] = of_chunk(chunk, b0)
            copies.append(pltpu.make_async_copy(held.at[:, c], out_ref.at[:, c], done.at[c]))
            copies[-1].start()
        for copy in copies:
            copy.wait()

    @pl.when(jnp.logical_not(late()))
    def _():
        factors = [[last_ref[o, i] for i in range(CHUNKS)] for o in range(CHUNKS)]
        size = BLOCKS // PARTS
        copies = []
        for part in range(PARTS):
            for block in range(part * size, part * size + size):
                for b7 in (0, 1):
                    tiles = [in_ref[seat(i), block, rows_of(b7)] for i in range(CHUNKS)]
                    for o in range(CHUNKS):
                        value = weighted(factors[o], tiles)
                        value = -value if outer_parity(block & 1, o >> 1, o & 1, b7) else value
                        held[block, o, rows_of(b7)] = value
            span = pl.ds(part * size, size)
            copies.append(pltpu.make_async_copy(held.at[span], out_ref.at[span], done.at[part]))
            copies[-1].start()
        for copy in copies:
            copy.wait()


VMEM = pl.BlockSpec(memory_space=pltpu.VMEM)
HBM = pl.BlockSpec(memory_space=pltpu.HBM)
BY_CHUNK = (CHUNKS, BLOCKS, ROWS, LANES)
NATURAL = (BLOCKS, CHUNKS, ROWS, LANES)
CHUNK = (BLOCKS, ROWS, LANES)


BY_SPOT = (CHUNKS * BLOCKS, ROWS, LANES)
GROUP = ("h0", "x", "core", "h3", "z")


def f32(*shape):
    return jax.ShapeDtypeStruct(shape, jnp.float32)


def call(kernel, out_shape, *args, specs=None, out_specs=VMEM, scratch=(), flops=0, limit=16):
    return pl.pallas_call(
        kernel,
        out_shape=out_shape,
        in_specs=specs or [VMEM] * len(args),
        out_specs=out_specs,
        scratch_shapes=scratch,
        cost_estimate=pl.CostEstimate(flops=flops, bytes_accessed=2 * MIB, transcendentals=0),
        compiler_params=pltpu.CompilerParams(vmem_limit_bytes=limit * MIB),
    )(*args)


TABLE = f32(CHUNKS, CHUNKS, *TILE)


def first_call(angles, global_angles, state):
    shapes = (f32(*BY_SPOT), f32(*angles.shape), TABLE, f32(2, 2, *TILE), TABLE)
    args = [pltpu.with_memory_space_constraint(x, pltpu.HBM) for x in (angles, global_angles, state)]
    return call(
        first_kernel, tuple(pltpu.VMEM(x.shape, x.dtype) for x in shapes), *args, specs=[HBM] * 3, out_specs=(VMEM,) * 5,
        scratch=[
            pltpu.VMEM(angles.shape, jnp.float32),
            pltpu.VMEM(global_angles.shape, jnp.float32),
            pltpu.VMEM(state.shape, jnp.float32),
            pltpu.SemaphoreType.DMA((3,)),
        ],
        flops=1600 * MIB,
    )


def last_call(angles, last, amps):
    return call(
        last_kernel, f32(*NATURAL), angles, last, amps, out_specs=HBM,
        scratch=[pltpu.VMEM(NATURAL, jnp.float32), pltpu.SemaphoreType.DMA((PARTS,))],
    )


def on_device(state, layer_angles, global_angles):
    amps, angles, spin, sign, last = first_call(
        layer_angles.transpose(0, 2, 1, 3), global_angles.reshape(1, 2), state.reshape(NATURAL)
    )
    amps = lax.all_to_all(amps, GROUP, split_axis=0, concat_axis=0, tiled=True)
    amps = call(middle_kernel, f32(*BY_CHUNK), angles, spin, sign, amps, flops=1600 * MIB)
    amps = lax.all_to_all(
        amps.reshape(CHUNKS, BLOCKS * ROWS, LANES), ("h0", "h3"), split_axis=0, concat_axis=0, tiled=True
    )
    return last_call(angles, last, amps.reshape(BY_CHUNK)).reshape(state.shape)


def solution(mesh):
    high, low = mesh.shape["hi"], mesh.shape["lo"]
    sizes = (2, high // 4, 2, 4, low // 8, 2)
    finer = Mesh(mesh.devices.reshape(sizes), ("h3", "hm", "h0", "z", "x", "core"))
    spec = P(("h3", "hm", "h0"), ("z", "x", "core"), None)
    return jax.shard_map(on_device, mesh=finer, in_specs=(spec, P(), P()), out_specs=spec, check_vma=False)
```

```python
import functools

import jax
import jax.numpy as jnp
from jax import lax
from jax.experimental import pallas as pl
from jax.experimental.pallas import tpu as pltpu
from jax.sharding import Mesh
from jax.sharding import PartitionSpec as P

ROW_BITS = (1, 2, 3, 4, 7, 8, 9, 10)
COL_BITS = (0, 11, 12, 13, 14, 15, 16, 17)
SIDE = 256
CHUNKS = 4
BLOCKS = 32
ROWS = 16
LANES = 128
TILE = (8, LANES)
EVERY = [(o, i) for o in range(CHUNKS) for i in range(CHUNKS)]
MIB = 2**20
PARTS = 4


def trig(angles_ref, section, layer):
    half = angles_ref[section, :, layer] * 0.5
    cosines, sines = jnp.cos(half), jnp.sin(half)

    def of(bit):
        group, qubit = bit // 6, bit % 6
        return (
            cosines[group : group + 1, qubit : qubit + 1],
            sines[group : group + 1, qubit : qubit + 1],
        )

    return of


def bit_of(index, place):
    return (index >> place) & 1


def signs_of(parity):
    return (1 - 2 * (parity & 1)).astype(jnp.float32)


def ry(pair, out, inner):
    cosine, sine = pair
    if isinstance(out, int):
        return cosine if out == inner else sine if out == 1 else -sine
    return jnp.where(out == inner, cosine, jnp.where(out == 1, sine, -sine))


def gate(bits, of, transposed):
    row = lax.broadcasted_iota(jnp.int32, TILE, 0)
    lane = lax.broadcasted_iota(jnp.int32, TILE, 1)
    pairs = [(i, i + 1) for i in range(7) if bits[i] + 1 == bits[i + 1]]

    def entry(i, r, c):
        cosine, sine = of(bits[i])
        out, inner = (c, r) if transposed else (r, c)
        if isinstance(c, int):
            return ry((cosine, sine), out, inner)
        return jnp.where(r == c, cosine, jnp.where(out == 1, sine, -sine))

    if transposed:
        out_bit = {i: bit_of(lane, 7 - i) for i in range(1, 8)}
    else:
        out_bit = {i: bit_of(row, 7 - i) for i in range(5, 8)}
    base = jnp.ones(TILE, jnp.float32)
    for i in (5, 6, 7):
        base = base * entry(i, bit_of(row, 7 - i), bit_of(lane, 7 - i))
    parity = jnp.zeros(TILE, jnp.int32)
    for i, j in pairs:
        if i in out_bit and j in out_bit:
            parity = parity + out_bit[i] * out_bit[j]
    tiles = {(): base * signs_of(parity)}
    for i in (4, 3, 2, 1):
        grown = {}
        for r in (0, 1):
            factor = entry(i, r, bit_of(lane, 7 - i))
            if not transposed and r == 1 and (i, i + 1) in pairs and i + 1 in out_bit:
                factor = factor * signs_of(out_bit[i + 1])
            for key, tile in tiles.items():
                grown[(r, *key)] = tile * factor
        tiles = grown
    halves = []
    for c in (0, 1):
        column = {}
        for r in (0, 1):
            factor = entry(0, r, c)
            if transposed and c == 1 and (0, 1) in pairs:
                factor = factor * signs_of(out_bit[1])
            for key, tile in tiles.items():
                column[(r, *key)] = tile * factor
        if not transposed:
            for key in column:
                if sum(key[i] * key[j] for i, j in pairs if j < 5) % 2:
                    column[key] = -column[key]
        halves.append(jnp.concatenate([column[key] for key in sorted(column)], axis=0))
    return jnp.concatenate(halves, axis=1)


def split(value):
    high = value.astype(jnp.bfloat16)
    low = (value - high.astype(jnp.float32)).astype(jnp.bfloat16)
    return high, low


def dot3(left, right):
    mul = functools.partial(jnp.dot, preferred_element_type=jnp.float32)
    return mul(left[0], right[0]) + mul(left[0], right[1]) + mul(left[1], right[0])


def section_gates(angles_ref, section):
    gates = []
    for layer in (0, 1):
        of = trig(angles_ref, section, layer)
        gates.append(split(gate(COL_BITS, of, True)))
        gates.append(split(gate(ROW_BITS, of, False)))
    return gates


def edge_tile():
    row = lax.broadcasted_iota(jnp.int32, TILE, 0)
    lane = lax.broadcasted_iota(jnp.int32, TILE, 1)
    return signs_of(bit_of(row, 0) * bit_of(lane, 6))


def chunk_sign(tile_of):
    tiles = {(b4, b7): tile_of(b4, b7) for b4 in (0, 1) for b7 in (0, 1)}
    columns = []
    for b0 in (0, 1):
        column = []
        for upper in range(16):
            for b7 in (0, 1):
                tile = tiles[upper & 1, b7]
                column.append(-tile if b0 and upper >= 8 else tile)
        columns.append(jnp.concatenate(column, axis=0))
    return jnp.concatenate(columns, axis=1)


def chunk_layers(chunks, gates, signs0, sign1):
    right0, left0, right1, left1 = gates
    chunks = [dot3(split(chunk), right0) for chunk in chunks]
    chunks = [dot3(left0, split(chunk)) * sign for chunk, sign in zip(chunks, signs0, strict=True)]
    chunks = [dot3(split(chunk), right1) for chunk in chunks]
    chunks = [dot3(left1, split(chunk)) for chunk in chunks]
    return chunks if sign1 is None else [chunk * sign1 for chunk in chunks]


def weighted(factors, values):
    total = None
    for factor, value in zip(factors, values, strict=True):
        term = factor * value
        total = term if total is None else total + term
    return total


def to_chunk(pieces):
    return jnp.concatenate([piece.reshape(SIDE, LANES) for piece in pieces], axis=1)


def of_chunk(chunk, half):
    return chunk[:, half * LANES : (half + 1) * LANES].reshape(16, ROWS, LANES)


def halves(half):
    return slice(half * 16, half * 16 + 16)


def spot(c, block):
    z, x, core = block // 8, block // 2 % 4, block % 2
    return (((c % 2) * 4 + x) * 2 + core) * 8 + (c // 2) * 4 + z


def rows_of(b7):
    return slice(b7 * 8, b7 * 8 + 8)


def outer_parity(b4, b5, b6, b7):
    return (b4 * b5 + b5 * b6 + b6 * b7) % 2


def pair_of(first, second, out, inner):
    return ry(first, out >> 1, inner >> 1) * ry(second, out & 1, inner & 1)


def prepare_first(angles_ref):
    gates = section_gates(angles_ref, 0)
    angles = [trig(angles_ref, *at) for at in ((0, 0), (0, 1), (1, 0))]
    fives, sixes = [of(5) for of in angles], [of(6) for of in angles]
    enter = [[pair_of(fives[0], sixes[0], o, i) for i in range(CHUNKS)] for o in range(CHUNKS)]
    before = {(o, i): pair_of(fives[1], sixes[1], o, i) for o, i in EVERY}
    after = {(o, i): pair_of(fives[2], sixes[2], o, i) for o, i in EVERY}
    leave = {(b4, b7): [[None] * CHUNKS for _ in range(CHUNKS)] for b4 in (0, 1) for b7 in (0, 1)}
    for o, i in EVERY:
        terms = [after[o, k] * before[k, i] for k in range(CHUNKS)]
        for (b4, b7), table in leave.items():
            total = None
            for k, term in enumerate(terms):
                term = -term if outer_parity(b4, k >> 1, k & 1, b7) else term
                total = term if total is None else total + term
            table[o][i] = jnp.broadcast_to(total, TILE)
    return gates, enter, leave


def prepare_next(angles_ref, global_ref, kept_ref, spin_ref, sign_ref, last_ref):
    kept_ref[...] = angles_ref[...]
    later = trig(angles_ref, 1, 1)
    half = global_ref[...] * 0.5
    cosines, sines = jnp.cos(half), jnp.sin(half)
    low, high = ((cosines[:, i : i + 1], sines[:, i : i + 1]) for i in (0, 1))
    for o, i in EVERY:
        spin_ref[o, i] = jnp.broadcast_to(pair_of(high, low, o, i), TILE)
        last_ref[o, i] = jnp.broadcast_to(pair_of(later(5), later(6), o, i), TILE)
    edge = edge_tile()
    place5, place6 = lax.axis_index("h3"), lax.axis_index("h0")
    sign5, sign6, both = signs_of(place5), signs_of(place6), signs_of(place5 * place6)
    for b4 in (0, 1):
        for b7 in (0, 1):
            factor = both
            if b4:
                factor = factor * sign5
            if b7:
                factor = factor * sign6
            sign_ref[b4, b7] = edge * factor


def mixed_chunk(factors, pieces):
    return to_chunk([weighted(factors, [pieces(k, half) for k in range(CHUNKS)]) for half in (0, 1)])


def first_kernel(angles_ref, global_ref, state_ref, out_ref, *refs):
    *next_refs, angles, spins, held, done = refs
    copies = [
        pltpu.make_async_copy(source, target, done.at[at])
        for at, (source, target) in enumerate([(angles_ref, angles), (global_ref, spins), (state_ref, held)])
    ]
    for copy in copies:
        copy.start()
    copies[0].wait()
    gates, enter, leave = prepare_first(angles)
    edge = edge_tile()
    copies[1].wait()
    prepare_next(angles, spins, *next_refs)
    copies[2].wait()
    chunks, signs0 = [], []
    for c in range(CHUNKS):
        chunks.append(mixed_chunk(enter[c], lambda k, half: held[halves(half), k]))
        signs0.append(outer_signs(edge, c))
    chunks = chunk_layers(chunks, gates, signs0, None)
    for c, chunk in enumerate(chunks):
        for b0 in (0, 1):
            piece = of_chunk(chunk, b0)
            for at in range(16):
                out_ref[spot(c, b0 * 16 + at)] = piece[at]
    for (b4, b7), factors in leave.items():
        plain = [[factor * edge for factor in line] for line in factors]
        turned = [[-factor for factor in line] for line in plain]
        for block in range(b4, BLOCKS, 2):
            tiles = [out_ref[spot(i, block), rows_of(b7)] for i in range(CHUNKS)]
            for o in range(CHUNKS):
                out_ref[spot(o, block), rows_of(b7)] = weighted((turned if block >= 24 else plain)[o], tiles)


def late():
    return lax.axis_index("core") == 1


def outer_signs(edge, c):
    return chunk_sign(lambda b4, b7: -edge if outer_parity(b4, c >> 1, c & 1, b7) else edge)


def middle_kernel(angles_ref, spin_ref, sign_ref, in_ref, out_ref):
    @pl.when(late())
    def _():
        factors = [[spin_ref[o, i] for i in range(CHUNKS)] for o in range(CHUNKS)]
        for block in range(BLOCKS):
            for b7 in (0, 1):
                tiles = [in_ref[spot(i, block), rows_of(b7)] for i in range(CHUNKS)]
                for o in range(CHUNKS):
                    out_ref[o, block, rows_of(b7)] = weighted(factors[o], tiles)

    @pl.when(jnp.logical_not(late()))
    def _():
        def half_of(k, half):
            return jnp.stack([in_ref[spot(k, half * 16 + at)] for at in range(16)])

        factors = [[jnp.concatenate([spin_ref[o, i]] * 2, axis=0)[None] for i in range(CHUNKS)] for o in range(CHUNKS)]
        chunks = [mixed_chunk(factors[c], half_of) for c in range(CHUNKS)]
        edge = edge_tile()
        sign0 = chunk_sign(lambda b4, b7: sign_ref[b4, b7])
        chunks = chunk_layers(chunks, section_gates(angles_ref, 1), [sign0] * CHUNKS, chunk_sign(lambda b4, b7: edge))
        for c, chunk in enumerate(chunks):
            for b0 in (0, 1):
                out_ref[c, halves(b0)] = of_chunk(chunk, b0)


def last_kernel(angles_ref, last_ref, in_ref, out_ref, held, done):
    @pl.when(late())
    def _():
        right0, left0, right1, left1 = section_gates(angles_ref, 1)
        edge = edge_tile()
        chunks = [to_chunk([in_ref[c, halves(b0)] for b0 in (0, 1)]) for c in range(CHUNKS)]
        chunks = [dot3(split(chunk), right0) for chunk in chunks]
        chunks = [dot3(left0, split(chunk)) * outer_signs(edge, c) for c, chunk in enumerate(chunks)]
        factors = [[last_ref[o, i][0:1, 0:1] for i in range(CHUNKS)] for o in range(CHUNKS)]
        chunks = [weighted(factors[o], chunks) for o in range(CHUNKS)]
        chunks = [dot3(split(chunk), right1) for chunk in chunks]
        copies = []
        for c, chunk in enumerate(chunks):
            chunk = dot3(left1, split(chunk)) * outer_signs(edge, c)
            for b0 in (0, 1):
                held[halves(b0), c] = of_chunk(chunk, b0)
            copies.append(pltpu.make_async_copy(held.at[:, c], out_ref.at[:, c], done.at[c]))
            copies[-1].start()
        for copy in copies:
            copy.wait()

    @pl.when(jnp.logical_not(late()))
    def _():
        factors = [[last_ref[o, i] for i in range(CHUNKS)] for o in range(CHUNKS)]
        size = BLOCKS // PARTS
        copies = []
        for part in range(PARTS):
            for block in range(part * size, part * size + size):
                for b7 in (0, 1):
                    tiles = [in_ref[i, block, rows_of(b7)] for i in range(CHUNKS)]
                    for o in range(CHUNKS):
                        value = weighted(factors[o], tiles)
                        value = -value if outer_parity(block & 1, o >> 1, o & 1, b7) else value
                        held[block, o, rows_of(b7)] = value
            span = pl.ds(part * size, size)
            copies.append(pltpu.make_async_copy(held.at[span], out_ref.at[span], done.at[part]))
            copies[-1].start()
        for copy in copies:
            copy.wait()


VMEM = pl.BlockSpec(memory_space=pltpu.VMEM)
HBM = pl.BlockSpec(memory_space=pltpu.HBM)
BY_CHUNK = (CHUNKS, BLOCKS, ROWS, LANES)
NATURAL = (BLOCKS, CHUNKS, ROWS, LANES)
CHUNK = (BLOCKS, ROWS, LANES)


BY_SPOT = (CHUNKS * BLOCKS, ROWS, LANES)
GROUP = ("h0", "x", "core", "h3", "z")


def f32(*shape):
    return jax.ShapeDtypeStruct(shape, jnp.float32)


def call(kernel, out_shape, *args, specs=None, out_specs=VMEM, scratch=(), flops=0, limit=16):
    return pl.pallas_call(
        kernel,
        out_shape=out_shape,
        in_specs=specs or [VMEM] * len(args),
        out_specs=out_specs,
        scratch_shapes=scratch,
        cost_estimate=pl.CostEstimate(flops=flops, bytes_accessed=2 * MIB, transcendentals=0),
        compiler_params=pltpu.CompilerParams(vmem_limit_bytes=limit * MIB),
    )(*args)


TABLE = f32(CHUNKS, CHUNKS, *TILE)


def first_call(angles, global_angles, state):
    shapes = (f32(*BY_SPOT), f32(*angles.shape), TABLE, f32(2, 2, *TILE), TABLE)
    args = [pltpu.with_memory_space_constraint(x, pltpu.HBM) for x in (angles, global_angles, state)]
    return call(
        first_kernel, tuple(pltpu.VMEM(x.shape, x.dtype) for x in shapes), *args, specs=[HBM] * 3, out_specs=(VMEM,) * 5,
        scratch=[
            pltpu.VMEM(angles.shape, jnp.float32),
            pltpu.VMEM(global_angles.shape, jnp.float32),
            pltpu.VMEM(state.shape, jnp.float32),
            pltpu.SemaphoreType.DMA((3,)),
        ],
        flops=1600 * MIB,
    )


def last_call(angles, last, amps):
    return call(
        last_kernel, f32(*NATURAL), angles, last, amps, out_specs=HBM,
        scratch=[pltpu.VMEM(NATURAL, jnp.float32), pltpu.SemaphoreType.DMA((PARTS,))],
    )


def on_device(state, layer_angles, global_angles):
    amps, angles, spin, sign, last = first_call(
        layer_angles.transpose(0, 2, 1, 3), global_angles.reshape(1, 2), state.reshape(NATURAL)
    )
    amps = lax.all_to_all(amps, GROUP, split_axis=0, concat_axis=0, tiled=True)
    amps = call(middle_kernel, f32(*BY_CHUNK), angles, spin, sign, amps, flops=1600 * MIB)
    amps = lax.all_to_all(
        amps.reshape(CHUNKS, BLOCKS * ROWS, LANES), ("h3", "h0"), split_axis=0, concat_axis=0, tiled=True
    )
    return last_call(angles, last, amps.reshape(BY_CHUNK)).reshape(state.shape)


def solution(mesh):
    high, low = mesh.shape["hi"], mesh.shape["lo"]
    sizes = (2, high // 4, 2, 4, low // 8, 2)
    finer = Mesh(mesh.devices.reshape(sizes), ("h3", "hm", "h0", "z", "x", "core"))
    spec = P(("h3", "hm", "h0"), ("z", "x", "core"), None)
    return jax.shard_map(on_device, mesh=finer, in_specs=(spec, P(), P()), out_specs=spec, check_vma=False)
```
